256 devices in a mesh: space: 8 (over x, y_lo), snap: 32 (over y_hi, z, core).
Axes of the slice: x: 4, y: 4 (y_hi: 2, y_lo: 2; y = y_hi * 2 + y_lo), z: 8, core: 2. Of those that a mesh axis runs over, the one named last changes fastest.
Arguments:
- snapshots: bfloat16 [8192, 131072], P('space', 'snap'), may hold values from -6 to 6
- vectors_cyclic: float32 [131072, 64], P('snap', 'space'), may hold values from -0.015625 to 0.015625
- eigen_values: float32 [64], replicated, may hold values from 0.25 to 25
- held_out: bfloat16 [8192, 256], P(('space', 'snap')), may hold values from -6 to 6
Outputs:
- modes: bfloat16 [8192, 64], P(('space', 'snap'))
- coefficients: float32 [64, 256], replicated
The draws below stay inside these ranges and needn't reach their ends.
All inputs are finite; a program needn't handle non-finite values.
Results may differ from the reference program's by a relative error of at most 0.0052.
Values sent between devices are 32-bit elements; how exact they have to be, the bound alone decides.
A program may use at most 64 MiB of HBM per device.

```python
import math
import jax
import jax.numpy as jnp
from jax import lax

MODES = 64
SNAP_DEV = 4096
HELD = 256
ROW_BLOCK = 16
COL_BLOCK = 4
CELLS = 8192
SNAPS = 131072
N_SPACE = 8
N_SNAP = 32


def raised(entries, rng, source, target, blocks, factor):
    def block_of(dim):
        return (jnp.arange(entries.shape[dim]) // (entries.shape[dim] // blocks)).reshape((-1,) + (1,) * (entries.ndim - 1 - dim))

    one_side = jax.random.permutation(rng, blocks)[block_of(target)]
    second = (block_of(target) + blocks // 2) % blocks
    return jnp.where((block_of(source) == one_side) | (block_of(source) == second), factor * entries, entries)


def steps_of(key, dims, pieces, low, largest):
    factor_of, own = 1.0, jax.random.fold_in(key, 6)
    for axis_at, blocks in pieces:
        steps = jnp.exp(jax.random.uniform(jax.random.fold_in(own, axis_at), (blocks,), jnp.float32, low / len(pieces), largest / len(pieces)))
        factor_of = factor_of * jnp.repeat(steps, dims[axis_at] // blocks).reshape([-1 if axis == axis_at else 1 for axis in range(len(dims))])
    return factor_of


def noise(stream_key, shape, scale, bound, split=(), held_as=jnp.bfloat16):
    gain = steps_of(stream_key, shape, split, -0.22, 0.18) if split else 1.0
    values = jax.random.normal(stream_key, shape, jnp.float32) * scale * gain
    return jnp.minimum(jnp.maximum(values, -bound), bound).astype(held_as)


def heavy_noise(key, dims, spread, reach, split, heavy, kind=jnp.bfloat16):
    result = spread * jax.random.normal(key, dims, jnp.float32)
    if split:
        result = result * steps_of(key, dims, split, -0.22, 0.18)
    return jnp.clip(raised(result, jax.random.fold_in(key, 3), *heavy), -reach, reach).astype(kind)


def setup_inputs(seed: int = 0) -> dict:
    key_of = jax.random.split(jax.random.key(seed), 5)
    snapshots = heavy_noise(key_of[0], (CELLS, SNAPS), 1.0, 6.0, ((0, 8), (1, 32)), (1, 0, 32, 2.75))
    vectors_cyclic = noise(key_of[1], (SNAPS, MODES), SNAPS ** -0.5, 0.015625, ((0, 32), (1, 8)), jnp.float32)
    eigen_values = jnp.clip(jnp.exp(jax.random.uniform(key_of[2], (MODES,), jnp.float32, math.log(0.25), math.log(25.0))), 0.25, 25.0)
    held_out = noise(key_of[3], (CELLS, HELD), 1.0, 6.0, ((0, 256),))
    return dict(snapshots=snapshots, vectors_cyclic=vectors_cyclic, eigen_values=eigen_values, held_out=held_out)


def reference(snapshots, vectors_cyclic, eigen_values, held_out):
    eigvec = vectors_cyclic.reshape(N_SNAP, SNAP_DEV // ROW_BLOCK, ROW_BLOCK, MODES)
    eigvec = eigvec.transpose(1, 0, 2, 3).reshape(SNAPS, MODES)
    eigvec = eigvec.reshape(SNAPS, N_SPACE, MODES // (N_SPACE * COL_BLOCK), COL_BLOCK)
    eigvec = eigvec.transpose(0, 2, 1, 3).reshape(SNAPS, MODES)
    scaled = (eigvec * lax.rsqrt(eigen_values)[None, :]).astype(jnp.bfloat16)
    modes = jnp.dot(snapshots, scaled, preferred_element_type=jnp.float32).astype(jnp.bfloat16)
    coefficients = lax.dot_general(modes, held_out, (((0,), (0,)), ((), ())), preferred_element_type=jnp.float32)
    coefficients = coefficients / math.sqrt(CELLS)
    return (modes, coefficients)
```

```python
import functools
import math

import jax
import jax.numpy as jnp
from jax import lax
from jax.experimental import pallas as pl
from jax.experimental.pallas import tpu as pltpu
from jax.sharding import PartitionSpec as P

MESH = pl.DeviceIdType.MESH
ROW_BLOCK = 16
COL_BLOCK = 4
LANES = 128
SUBLANES = 8
CORES = 2
CHUNKS = 4
ROW_TILE = 256


def swap_lane_groups(tiles):
    count = len(tiles)
    lane = lax.broadcasted_iota(jnp.int32, tiles[0].shape, tiles[0].ndim - 1)
    step = 1
    while step < count:
        low = (lane // (ROW_BLOCK * step)) % 2 == 0
        fresh = list(tiles)
        for a in range(count):
            if a & step:
                continue
            x, y = tiles[a], tiles[a + step]
            fresh[a] = jnp.where(low, x, pltpu.roll(y, ROW_BLOCK * step, y.ndim - 1))
            fresh[a + step] = jnp.where(low, pltpu.roll(x, LANES - ROW_BLOCK * step, x.ndim - 1), y)
        tiles = fresh
        step *= 2
    return tiles


def mode_rows(held_rows, pairs):
    first, second = [], []
    for t in range(pairs):
        even, odd = held_rows[2 * t], held_rows[2 * t + 1]
        upper = lax.broadcasted_iota(jnp.int32, even.shape, 0) < COL_BLOCK
        first.append(jnp.where(upper, even, pltpu.roll(odd, COL_BLOCK, 0)))
        second.append(jnp.where(upper, pltpu.roll(even, COL_BLOCK, 0), odd))
    return jnp.concatenate(first + second, axis=0)


def kernel(
    n_space, n_snap, total_cells,
    s_hbm, v_hbm, ev_ref, h_hbm,
    modes_ref, coef_ref,
    s_v, h_v, recv, e_all, acc, pack, sums, c_out, c_in, d_out, d_in, f_in,
    s_sem, h_sem, a_send, a_recv, g_send, g_recv, r_send, r_recv, c_send, c_recv,
):
    q, p = lax.axis_index("space"), lax.axis_index("snap")
    core = lax.rem(p, CORES)
    n_near, n_far = n_space * CORES, n_snap // CORES
    near, far = q * CORES + core, p // CORES
    cells, snaps = s_v.shape
    modes = acc.shape[1]
    width = snaps // CHUNKS
    rows_each = cells // n_snap

    def near_id(a):
        return (a // CORES, p - core + lax.rem(a, CORES))

    def far_id(b):
        return (q, b * CORES + core)

    def s_copy(c):
        cols = pl.ds(c * width, width)
        return pltpu.make_async_copy(s_hbm.at[:, cols], s_v.at[:, cols], s_sem.at[c])

    def drain(view, sem):
        pltpu.make_async_copy(view, view, sem).wait()

    barrier = pltpu.get_barrier_semaphore()

    @pl.loop(1, n_snap)
    def _(d):
        pl.semaphore_signal(barrier, inc=1, device_id=(q, lax.rem(p + d, n_snap)), device_id_type=MESH)

    @pl.loop(1, n_space)
    def _(d):
        other = lax.rem(q + d, n_space)
        pl.semaphore_signal(barrier, inc=1, device_id=(other, p), device_id_type=MESH)
        pl.semaphore_signal(barrier, inc=1, device_id=(other, p + 1 - 2 * core), device_id_type=MESH)

    h_copy = pltpu.make_async_copy(h_hbm, h_v, h_sem)
    for c in range(CHUNKS):
        s_copy(c).start()
    h_copy.start()
    pl.semaphore_wait(barrier, n_snap - 1 + 2 * (n_space - 1))

    @pl.loop(1, n_snap)
    def _(d):
        other = lax.rem(p + d, n_snap)
        pltpu.make_async_remote_copy(
            src_ref=v_hbm.at[:, pl.ds(pl.multiple_of(other * LANES, LANES), LANES)],
            dst_ref=recv.at[p],
            send_sem=a_send,
            recv_sem=a_recv,
            device_id=(q, other),
            device_id_type=MESH,
        ).start()

    own = pltpu.make_async_copy(v_hbm.at[:, pl.ds(pl.multiple_of(p * LANES, LANES), LANES)], recv.at[p], c_send.at[3])
    own.start()
    row = lax.broadcasted_iota(jnp.int32, (SUBLANES, LANES), 0)
    values = jnp.zeros((SUBLANES, LANES), jnp.float32)
    for r in range(SUBLANES):
        value = ev_ref[((r // COL_BLOCK) * n_space + q) * COL_BLOCK + r % COL_BLOCK]
        values = jnp.where(row == r, value, values)
    scale = lax.rsqrt(values)
    own.wait()
    drain(recv.at[pl.ds(0, n_snap - 1)], a_recv)

    groups = LANES // ROW_BLOCK
    for g in range(n_snap // groups):
        tiles = swap_lane_groups([recv[g * groups + a] for a in range(groups)])
        for k in range(groups):
            at = k * n_snap * ROW_BLOCK + g * LANES
            e_all[q, :, at : at + LANES] = tiles[k] * scale

    for c in range(CHUNKS):
        cols = pl.ds(c * width, width)

        @pl.loop(1, n_space)
        def _(d):
            pltpu.make_async_remote_copy(
                src_ref=e_all.at[q, :, cols],
                dst_ref=e_all.at[q, :, cols],
                send_sem=g_send,
                recv_sem=g_recv.at[c],
                device_id=(lax.rem(q + d, n_space), p),
                device_id_type=MESH,
            ).start()

    tiles_m = cells // ROW_TILE
    targets = ROW_TILE // rows_each
    mine = p // targets
    for c in range(CHUNKS):
        cols = pl.ds(c * width, width)
        drain(e_all.at[pl.ds(0, n_space - 1), :, cols], g_recv.at[c])
        weights = mode_rows([e_all[s, :, cols] for s in range(n_space)], n_space // 2).astype(jnp.bfloat16)
        s_copy(c).wait()

        @pl.loop(0, tiles_m)
        def _(step):
            m = lax.rem(mine + 1 + step, tiles_m)
            rows = pl.ds(pl.multiple_of(m * ROW_TILE, ROW_TILE), ROW_TILE)
            value = lax.dot_general(
                s_v[rows, cols], weights, (((1,), (1,)), ((), ())), preferred_element_type=jnp.float32
            )
            if c > 0:
                value = value + acc[rows, :]
            if c < CHUNKS - 1:
                acc[rows, :] = value
            else:
                halves = value.reshape(targets, 2, rows_each // 2, modes)
                pack[pl.ds(m * targets, targets)] = jnp.concatenate([halves[:, 0], halves[:, 1]], axis=-1)

                @pl.loop(0, targets)
                def _(t):
                    other = m * targets + t

                    @pl.when(other != p)
                    def _():
                        pltpu.make_async_remote_copy(
                            src_ref=pack.at[other],
                            dst_ref=sums.at[p],
                            send_sem=r_send,
                            recv_sem=r_recv,
                            device_id=(q, other),
                            device_id_type=MESH,
                        ).start()

    sums[p] = pack[p]
    drain(sums.at[pl.ds(0, n_snap - 1)], r_recv)
    total = jnp.sum(sums[...], axis=0)
    found = jnp.concatenate([total[:, :modes], total[:, modes:]], axis=0).astype(jnp.bfloat16)
    modes_ref[...] = found

    h_copy.wait()
    partial_value = lax.dot_general(
        found, h_v[...], (((0,), (0,)), ((), ())), preferred_element_type=jnp.float32
    )
    wide = h_v.shape[1] // LANES
    for a in range(n_near):
        r, s = a // wide, a % wide
        c_out[a] = partial_value[r * SUBLANES : (r + 1) * SUBLANES, s * LANES : (s + 1) * LANES]

    @pl.loop(1, n_near)
    def _(d):
        other = lax.rem(near + d, n_near)
        pltpu.make_async_remote_copy(
            src_ref=c_out.at[other],
            dst_ref=c_in.at[near],
            send_sem=c_send.at[0],
            recv_sem=c_recv.at[0],
            device_id=near_id(other),
            device_id_type=MESH,
        ).start()

    c_in[near] = c_out[near]
    drain(c_in.at[pl.ds(0, n_near - 1)], c_recv.at[0])
    d_out[...] = jnp.sum(c_in[...], axis=0)

    @pl.loop(1, n_far)
    def _(d):
        pltpu.make_async_remote_copy(
            src_ref=d_out,
            dst_ref=d_in.at[far],
            send_sem=c_send.at[1],
            recv_sem=c_recv.at[1],
            device_id=far_id(lax.rem(far + d, n_far)),
            device_id_type=MESH,
        ).start()

    d_in[far] = d_out[...]
    drain(d_in.at[pl.ds(0, n_far - 1)], c_recv.at[1])
    f_in[near] = jnp.sum(d_in[...], axis=0) * (1.0 / math.sqrt(total_cells))

    @pl.loop(1, n_near)
    def _(d):
        pltpu.make_async_remote_copy(
            src_ref=f_in.at[near],
            dst_ref=f_in.at[near],
            send_sem=c_send.at[2],
            recv_sem=c_recv.at[2],
            device_id=near_id(lax.rem(near + d, n_near)),
            device_id_type=MESH,
        ).start()

    drain(recv.at[pl.ds(0, n_snap - 1)], a_send)
    for c in range(CHUNKS):
        drain(e_all.at[pl.ds(0, n_space - 1), :, pl.ds(c * width, width)], g_send)
    drain(pack.at[pl.ds(0, n_snap - 1)], r_send)
    drain(c_out.at[pl.ds(0, n_near - 1)], c_send.at[0])
    drain(d_in.at[pl.ds(0, n_far - 1)], c_send.at[1])
    drain(f_in.at[pl.ds(0, n_near - 1)], c_recv.at[2])
    for a in range(n_near):
        r, s = a // wide, a % wide
        coef_ref[r * SUBLANES : (r + 1) * SUBLANES, s * LANES : (s + 1) * LANES] = f_in[a]
    drain(f_in.at[pl.ds(0, n_near - 1)], c_send.at[2])


def solution(mesh):
    n_space, n_snap = mesh.shape["space"], mesh.shape["snap"]

    def per_device(snapshots, vectors_cyclic, eigen_values, held_out):
        cells, snaps = snapshots.shape
        modes, held = eigen_values.shape[0], held_out.shape[1]
        rows_each = cells // n_snap
        n_near, n_far = n_space * CORES, n_snap // CORES
        tile = (SUBLANES, LANES)
        vmem, dma = pltpu.VMEM, pltpu.SemaphoreType.DMA
        f32 = jnp.float32
        return pl.pallas_call(
            functools.partial(kernel, n_space, n_snap, cells * n_space),
            out_shape=(
                jax.ShapeDtypeStruct((rows_each, modes), jnp.bfloat16),
                jax.ShapeDtypeStruct((modes, held), f32),
            ),
            in_specs=[
                pl.BlockSpec(memory_space=pl.ANY),
                pl.BlockSpec(memory_space=pl.ANY),
                pl.BlockSpec(memory_space=pltpu.SMEM),
                pl.BlockSpec(memory_space=pl.ANY),
            ],
            out_specs=[pl.BlockSpec(memory_space=pltpu.VMEM)] * 2,
            scratch_shapes=[
                vmem((cells, snaps), jnp.bfloat16),
                vmem(held_out.shape, jnp.bfloat16),
                vmem((n_snap, *tile), f32),
                vmem((n_space, SUBLANES, snaps), f32),
                vmem((cells, modes), f32),
                vmem((n_snap, rows_each // 2, 2 * modes), f32),
                vmem((n_snap, rows_each // 2, 2 * modes), f32),
                vmem((n_near, *tile), f32),
                vmem((n_near, *tile), f32),
                vmem(tile, f32),
                vmem((n_far, *tile), f32),
                vmem((n_near, *tile), f32),
                dma((CHUNKS,)),
                dma,
                dma,
                dma,
                dma,
                dma((CHUNKS,)),
                dma,
                dma,
                dma((4,)),
                dma((3,)),
            ],
            compiler_params=pltpu.CompilerParams(
                collective_id=0, has_side_effects=True, vmem_limit_bytes=60 * 1024 * 1024
            ),
        )(snapshots, vectors_cyclic.T, eigen_values, held_out)

    return jax.shard_map(
        per_device,
        mesh=mesh,
        in_specs=(P("space", "snap"), P("snap", "space"), P(), P(("space", "snap"), None)),
        out_specs=(P(("space", "snap"), None), P()),
        check_vma=False,
    )
```

```python
import functools
import math

import jax
import jax.numpy as jnp
from jax import lax
from jax.experimental import pallas as pl
from jax.experimental.pallas import tpu as pltpu
from jax.sharding import PartitionSpec as P

MESH = pl.DeviceIdType.MESH
ROW_BLOCK = 16
COL_BLOCK = 4
LANES = 128
SUBLANES = 8
CORES = 2
ROW_TILE = 256
VMEM_LIMIT = 57 * 1024 * 1024
ROUTES = ("x", "y", "x", "y")


def swap_lane_groups(tiles):
    count = len(tiles)
    lane = lax.broadcasted_iota(jnp.int32, tiles[0].shape, tiles[0].ndim - 1)
    step = 1
    while step < count:
        low = (lane // (ROW_BLOCK * step)) % 2 == 0
        fresh = list(tiles)
        for a in range(count):
            if a & step:
                continue
            x, y = tiles[a], tiles[a + step]
            fresh[a] = jnp.where(low, x, pltpu.roll(y, ROW_BLOCK * step, y.ndim - 1))
            fresh[a + step] = jnp.where(low, pltpu.roll(x, LANES - ROW_BLOCK * step, x.ndim - 1), y)
        tiles = fresh
        step *= 2
    return tiles


def mode_rows(held_rows, pairs):
    first, second = [], []
    for t in range(pairs):
        even, odd = held_rows[2 * t], held_rows[2 * t + 1]
        upper = lax.broadcasted_iota(jnp.int32, even.shape, 0) < COL_BLOCK
        first.append(jnp.where(upper, even, pltpu.roll(odd, COL_BLOCK, 0)))
        second.append(jnp.where(upper, pltpu.roll(even, COL_BLOCK, 0), odd))
    return jnp.concatenate(first + second, axis=0)


def kernel(
    n_space, n_snap, total_cells,
    s_hbm, v_hbm, ev_ref, h_hbm,
    modes_ref, coef_ref,
    s_v, h_v, h_all, recv, e_all, acc, pack, partner, paired, sums, c_out, c_in, d_out, d_in, f_in,
    s_sem, h_sem, a_send, a_recv, own_sem, hy_send, hy_recv, hz_send, hz_recv, g_send, g_first, g_rest,
    k_send, k_recv, r_send, r_recv, c_send, c_recv,
):
    q, p = lax.axis_index("space"), lax.axis_index("snap")
    core = lax.rem(p, CORES)
    n_near, n_far = n_space * CORES, n_snap // CORES
    near, far = q * CORES + core, p // CORES
    n_x, n_z = n_space // 2, n_far // 2
    x, y = q // 2, lax.rem(q, 2)
    z, row_y = lax.rem(far, n_z), far // n_z
    across = 2 * x + 1 - y
    facing = (1 - row_y) * n_z + z
    cells, snaps = s_v.shape
    modes = acc.shape[1]
    groups = LANES // ROW_BLOCK
    chunks = n_snap // groups
    half = max(chunks // 2, 1)
    rows_each = cells // n_snap
    tiles_m = cells // ROW_TILE
    owners = n_far // tiles_m

    def remote(src, dst, send, arrived, space, snap):
        return pltpu.make_async_remote_copy(
            src_ref=src, dst_ref=dst, send_sem=send, recv_sem=arrived, device_id=(space, snap), device_id_type=MESH
        )

    def drain(view, sem):
        pltpu.make_async_copy(view, view, sem).wait()

    def near_id(a):
        return a // CORES, p - core + lax.rem(a, CORES)

    def group_of(o):
        if chunks == 1:
            return 0
        own_y, own_z = p // groups // half, lax.rem(p // groups, half)
        return lax.rem(own_y + o // half, 2) * half + lax.rem(own_z + o % half, half)

    barrier = pltpu.get_barrier_semaphore()

    @pl.loop(1, n_snap)
    def _(d):
        pl.semaphore_signal(barrier, inc=1, device_id=(q, lax.rem(p + d, n_snap)), device_id_type=MESH)

    @pl.loop(1, n_space)
    def _(d):
        other = lax.rem(q + d, n_space)
        pl.semaphore_signal(barrier, inc=1, device_id=(other, p), device_id_type=MESH)
        pl.semaphore_signal(barrier, inc=1, device_id=(other, p + 1 - 2 * core), device_id_type=MESH)

    own = pltpu.make_async_copy(v_hbm.at[:, pl.ds(pl.multiple_of(p * LANES, LANES), LANES)], recv.at[p], own_sem)
    own.start()
    h_copy = pltpu.make_async_copy(h_hbm, h_v, h_sem)
    h_copy.start()

    def s_copy(m):
        rows = pl.ds(m * ROW_TILE, ROW_TILE)
        return pltpu.make_async_copy(s_hbm.at[rows], s_v.at[rows], s_sem.at[m])

    for m in range(tiles_m):
        s_copy(m).start()
    row = lax.broadcasted_iota(jnp.int32, (SUBLANES, LANES), 0)
    values = jnp.zeros((SUBLANES, LANES), jnp.float32)
    for r in range(SUBLANES):
        value = ev_ref[((r // COL_BLOCK) * n_space + q) * COL_BLOCK + r % COL_BLOCK]
        values = jnp.where(row == r, value, values)
    scale = lax.rsqrt(values)
    h_copy.wait()
    h_all[far] = h_v[...].astype(jnp.float32)
    own.wait()
    pl.semaphore_wait(barrier, n_snap - 1 + 2 * (n_space - 1))

    @pl.loop(1, n_snap)
    def _(d):
        other = lax.rem(p + d, n_snap)
        cols = pl.ds(pl.multiple_of(other * LANES, LANES), LANES)
        remote(v_hbm.at[:, cols], recv.at[p], a_send, a_recv.at[p // groups], q, other).start()

    remote(h_all.at[far], h_all.at[far], hy_send, hy_recv, q, facing * CORES + core).start()

    def order_chunk(o):
        group = group_of(o)
        drain(recv.at[pl.ds(0, groups - 1 if o == 0 else groups)], a_recv.at[group])
        tiles = swap_lane_groups([recv[group * groups + a] for a in range(groups)])
        for k in range(groups):
            e_all[q, o, :, k * LANES : (k + 1) * LANES] = tiles[k] * scale

    def send_rows(source, o, sem, space):
        remote(e_all.at[source, o], e_all.at[source, o], g_send, sem, space, p).start()

    def along_x(source, o, sem):
        @pl.loop(1, n_x)
        def _(d):
            send_rows(source, o, sem, 2 * lax.rem(x + d, n_x) + y)

    def start_chunk(o):
        route = ROUTES[o]
        if route == "d":

            @pl.loop(1, n_space)
            def _(d):
                send_rows(q, o, g_rest.at[o], lax.rem(q + d, n_space))

        elif route == "y":
            send_rows(q, o, g_first.at[o], across)
            along_x(q, o, g_rest.at[o])
        else:
            along_x(q, o, g_first.at[o])
            send_rows(q, o, g_rest.at[o], across)

    def relay_chunk(o):
        route = ROUTES[o]
        if route == "y":
            drain(e_all.at[0, o], g_first.at[o])
            along_x(across, o, g_rest.at[o])
        elif route == "x" and n_x > 1:
            drain(e_all.at[pl.ds(0, n_x - 1), o], g_first.at[o])

            @pl.loop(1, n_x)
            def _(d):
                send_rows(2 * lax.rem(x + d, n_x) + y, o, g_rest.at[o], across)

    def multiply_chunk(o):
        rest = {"d": n_space - 1, "y": 2 * (n_x - 1), "x": n_x}[ROUTES[o]]
        if rest:
            drain(e_all.at[pl.ds(0, rest), o], g_rest.at[o])
        weights = mode_rows([e_all[s, o] for s in range(n_space)], n_space // 2).astype(jnp.bfloat16)
        group = group_of(o)

        @pl.loop(0, tiles_m)
        def _(m):
            rows = pl.ds(pl.multiple_of(m * ROW_TILE, ROW_TILE), ROW_TILE)
            parts = []
            for k in range(groups):
                at = pl.multiple_of(k * n_snap * ROW_BLOCK + group * LANES, LANES)
                parts.append(s_v[rows, pl.ds(at, LANES)])
            value = lax.dot_general(
                jnp.concatenate(parts, axis=1), weights, (((1,), (1,)), ((), ())), preferred_element_type=jnp.float32
            )
            if o > 0:
                value = value + acc[rows, :]
            if o < chunks - 1:
                acc[rows, :] = value
            else:
                split = value.reshape(owners, CORES, 2, rows_each // 2, modes)
                mine = pl.ds(m * owners, owners)
                for c in range(CORES):
                    pack[c, mine] = jnp.concatenate([split[:, c, 0], split[:, c, 1]], axis=-1)
                remote(
                    pack.at[1 - core, mine], partner.at[mine], k_send, k_recv.at[m], q, p + 1 - 2 * core
                ).start()

    def send_held():
        drain(h_all.at[0], hy_recv)

        @pl.loop(1, n_z)
        def _(d):
            other = lax.rem(z + d, n_z) + row_y * n_z
            for slot in (far, facing):
                remote(h_all.at[slot], h_all.at[slot], hz_send, hz_recv, q, other * CORES + core).start()

    for o in range(chunks):
        order_chunk(o)
        start_chunk(o)
        if o == 0:
            send_held()
        if o >= 2:
            relay_chunk(o - 2)
    for o in range(max(chunks - 2, 0), chunks):
        relay_chunk(o)
        if o == chunks - 2:
            for m in range(tiles_m):
                s_copy(m).wait()
            multiply_chunk(0)
    if chunks == 1:
        for m in range(tiles_m):
            s_copy(m).wait()
        multiply_chunk(0)
    for o in range(1, chunks):
        multiply_chunk(o)

    @pl.loop(0, tiles_m)
    def _(m):
        mine = pl.ds(m * owners, owners)
        drain(partner.at[mine], k_recv.at[m])
        paired[mine] = pack[core, mine] + partner[mine]

        @pl.loop(0, owners)
        def _(t):
            other = m * owners + t

            @pl.when(other != far)
            def _():
                remote(paired.at[other], sums.at[far], r_send, r_recv, q, other * CORES + core).start()

    drain(h_all.at[pl.ds(0, 2 * (n_z - 1))], hz_recv)
    partial_value = None
    for s in range(2):
        found = paired[:, :, s * modes : (s + 1) * modes].reshape(n_far * rows_each // 2, modes)
        held = h_all[:, s * rows_each // 2 : (s + 1) * rows_each // 2, :].reshape(n_far * rows_each // 2, h_v.shape[1])
        held = held.astype(jnp.bfloat16)
        upper = found.astype(jnp.bfloat16)
        lower = (found - upper.astype(jnp.float32)).astype(jnp.bfloat16)
        for piece in (upper, lower):
            term = lax.dot_general(piece, held, (((0,), (0,)), ((), ())), preferred_element_type=jnp.float32)
            partial_value = term if partial_value is None else partial_value + term
    wide = h_v.shape[1] // LANES
    for a in range(n_near):
        r, s = a // wide, a % wide
        c_out[a] = partial_value[r * SUBLANES : (r + 1) * SUBLANES, s * LANES : (s + 1) * LANES]

    @pl.loop(1, n_near)
    def _(d):
        other = lax.rem(near + d, n_near)
        remote(c_out.at[other], c_in.at[near], c_send.at[0], c_recv.at[0], *near_id(other)).start()

    c_in[near] = c_out[near]
    drain(c_in.at[pl.ds(0, n_near - 1)], c_recv.at[0])
    d_out[...] = jnp.sum(c_in[...], axis=0)

    @pl.loop(1, n_far)
    def _(d):
        other = lax.rem(far + d, n_far)
        remote(d_out, d_in.at[far], c_send.at[1], c_recv.at[1], q, other * CORES + core).start()

    d_in[far] = d_out[...]
    sums[far] = paired[far]
    drain(sums.at[pl.ds(0, n_far - 1)], r_recv)
    modes_ref[...] = jnp.sum(sums[...], axis=0)
    drain(d_in.at[pl.ds(0, n_far - 1)], c_recv.at[1])
    f_in[near] = jnp.sum(d_in[...], axis=0) * (1.0 / math.sqrt(total_cells))

    @pl.loop(1, n_near)
    def _(d):
        other = lax.rem(near + d, n_near)
        remote(f_in.at[near], f_in.at[near], c_send.at[2], c_recv.at[2], *near_id(other)).start()

    drain(recv.at[pl.ds(0, n_snap - 1)], a_send)
    drain(h_all.at[0], hy_send)
    drain(h_all.at[pl.ds(0, 2 * (n_z - 1))], hz_send)
    for o in range(chunks):
        drain(e_all.at[pl.ds(0, n_space - 1), o], g_send)
    drain(partner, k_send)
    drain(sums.at[pl.ds(0, n_far - 1)], r_send)
    drain(c_out.at[pl.ds(0, n_near - 1)], c_send.at[0])
    drain(d_in.at[pl.ds(0, n_far - 1)], c_send.at[1])
    drain(f_in.at[pl.ds(0, n_near - 1)], c_recv.at[2])
    coef_ref[...] = f_in[...]
    drain(f_in.at[pl.ds(0, n_near - 1)], c_send.at[2])


def place(total_ref, tiles_ref, modes_ref, coef_ref):
    modes = modes_ref.shape[1]
    half = modes_ref.shape[0] // 2
    modes_ref[:half, :] = total_ref[:, :modes].astype(jnp.bfloat16)
    modes_ref[half:, :] = total_ref[:, modes:].astype(jnp.bfloat16)
    wide = coef_ref.shape[1] // LANES
    for a in range(tiles_ref.shape[0]):
        r, s = a // wide, a % wide
        coef_ref[r * SUBLANES : (r + 1) * SUBLANES, s * LANES : (s + 1) * LANES] = tiles_ref[a]


def solution(mesh):
    n_space, n_snap = mesh.shape["space"], mesh.shape["snap"]

    def per_device(snapshots, vectors_cyclic, eigen_values, held_out):
        cells, snaps = snapshots.shape
        modes, held = eigen_values.shape[0], held_out.shape[1]
        rows_each = cells // n_snap
        n_near, n_far = n_space * CORES, n_snap // CORES
        chunks = n_snap * ROW_BLOCK // LANES
        tile = (SUBLANES, LANES)
        packed = (rows_each // 2, 2 * modes)
        vmem, dma = pltpu.VMEM, pltpu.SemaphoreType.DMA
        f32 = jnp.float32
        total, tiles = pl.pallas_call(
            functools.partial(kernel, n_space, n_snap, cells * n_space),
            out_shape=(vmem(packed, f32), vmem((n_near, *tile), f32)),
            in_specs=[
                pl.BlockSpec(memory_space=pl.ANY),
                pl.BlockSpec(memory_space=pl.ANY),
                pl.BlockSpec(memory_space=pltpu.SMEM),
                pl.BlockSpec(memory_space=pl.ANY),
            ],
            out_specs=[pl.BlockSpec(memory_space=pltpu.VMEM)] * 2,
            scratch_shapes=[
                vmem((cells, snaps), jnp.bfloat16),
                vmem(held_out.shape, jnp.bfloat16),
                vmem((n_far, *held_out.shape), f32),
                vmem((n_snap, *tile), f32),
                vmem((n_space, chunks, SUBLANES, snaps // chunks), f32),
                vmem((cells, modes), f32),
                vmem((CORES, n_far, *packed), f32),
                vmem((n_far, *packed), f32),
                vmem((n_far, *packed), f32),
                vmem((n_far, *packed), f32),
                vmem((n_near, *tile), f32),
                vmem((n_near, *tile), f32),
                vmem(tile, f32),
                vmem((n_far, *tile), f32),
                vmem((n_near, *tile), f32),
                dma((cells // ROW_TILE,)),
                dma,
                dma,
                dma((chunks,)),
                dma,
                dma,
                dma,
                dma,
                dma,
                dma,
                dma((chunks,)),
                dma((chunks,)),
                dma,
                dma((cells // ROW_TILE,)),
                dma,
                dma,
                dma((3,)),
                dma((3,)),
            ],
            compiler_params=pltpu.CompilerParams(
                collective_id=0, has_side_effects=True, vmem_limit_bytes=VMEM_LIMIT
            ),
        )(snapshots, vectors_cyclic.T, eigen_values, held_out)
        return pl.pallas_call(
            place,
            out_shape=(
                jax.ShapeDtypeStruct((rows_each, modes), jnp.bfloat16),
                jax.ShapeDtypeStruct((modes, held), f32),
            ),
            in_specs=[pl.BlockSpec(memory_space=pltpu.VMEM)] * 2,
            out_specs=[pl.BlockSpec(memory_space=pltpu.VMEM)] * 2,
            compiler_params=pltpu.CompilerParams(vmem_limit_bytes=2 * 1024 * 1024),
        )(total, tiles)

    return jax.shard_map(
        per_device,
        mesh=mesh,
        in_specs=(P("space", "snap"), P("snap", "space"), P(), P(("space", "snap"), None)),
        out_specs=(P(("space", "snap"), None), P()),
        check_vma=False,
    )
```

```python
import functools
import math

import jax
import jax.numpy as jnp
from jax import lax
from jax.experimental import pallas as pl
from jax.experimental.pallas import tpu as pltpu
from jax.sharding import PartitionSpec as P

MESH = pl.DeviceIdType.MESH
ROW_BLOCK = 16
COL_BLOCK = 4
LANES = 128
SUBLANES = 8
CORES = 2
ROW_TILE = 256
VMEM_LIMIT = 57 * 1024 * 1024
OWN_ROUTES = ("x", "x")
OVER_ROUTES = ("y", "y")
HB_OWN = 2
HB_FACING = 3


def swap_lane_groups(tiles):
    count = len(tiles)
    lane = lax.broadcasted_iota(jnp.int32, tiles[0].shape, tiles[0].ndim - 1)
    step = 1
    while step < count:
        low = (lane // (ROW_BLOCK * step)) % 2 == 0
        fresh = list(tiles)
        for a in range(count):
            if a & step:
                continue
            x, y = tiles[a], tiles[a + step]
            fresh[a] = jnp.where(low, x, pltpu.roll(y, ROW_BLOCK * step, y.ndim - 1))
            fresh[a + step] = jnp.where(low, pltpu.roll(x, LANES - ROW_BLOCK * step, x.ndim - 1), y)
        tiles = fresh
        step *= 2
    return tiles


def mode_rows(held_rows, pairs):
    first, second = [], []
    for t in range(pairs):
        even, odd = held_rows[2 * t], held_rows[2 * t + 1]
        upper = lax.broadcasted_iota(jnp.int32, even.shape, 0) < COL_BLOCK
        first.append(jnp.where(upper, even, pltpu.roll(odd, COL_BLOCK, 0)))
        second.append(jnp.where(upper, pltpu.roll(even, COL_BLOCK, 0), odd))
    return jnp.concatenate(first + second, axis=0)


def kernel(
    n_space, n_snap, total_cells,
    s_hbm, v_hbm, ev_hbm, h_hbm,
    modes_ref, coef_ref,
    s_v, h_v, ev_ref, h_all, recv, staged, e_all, acc, pack, partner, paired, sums, c_out, c_in, d_out, d_in, f_in,
    s_sem, h_sem, ev_sem, a_send, a_recv, own_sem, hy_send, hy_recv, hz_send, hz_first, hz_rest, g_send, g_first, g_rest,
    k_send, k_recv, r_send, r_recv, c_send, c_recv,
):
    q, p = lax.axis_index("space"), lax.axis_index("snap")
    core = lax.rem(p, CORES)
    n_near, n_far = n_space * 2, n_snap // 2
    far = p // CORES
    n_x, n_z = n_space // 2, n_far // 2
    x, y = q // 2, lax.rem(q, 2)
    z, row_y = lax.rem(far, n_z), far // n_z
    across = 2 * x + 1 - y
    facing = (1 - row_y) * n_z + z
    near, line = row_y * n_space + q, z * CORES + core
    cells, snaps = s_v.shape
    modes = acc.shape[1]
    groups = LANES // ROW_BLOCK
    chunks = n_snap // groups
    parts = chunks // 2
    rows_each = cells // n_snap
    tiles_m = cells // ROW_TILE
    owners = n_far // tiles_m

    def remote(src, dst, send, arrived, space, snap):
        return pltpu.make_async_remote_copy(
            src_ref=src, dst_ref=dst, send_sem=send, recv_sem=arrived, device_id=(space, snap), device_id_type=MESH
        )

    def drain(view, sem):
        pltpu.make_async_copy(view, view, sem).wait()

    def near_id(a):
        return lax.rem(a, n_space), (a // n_space) * n_far + line

    def part_of(i):
        return lax.rem(line // groups + i, parts)

    def group_of(o):
        t, i = o // parts, o % parts
        return lax.rem(row_y + t, 2) * parts + part_of(i)

    barrier = pltpu.get_barrier_semaphore()

    @pl.loop(1, n_snap)
    def _(d):
        pl.semaphore_signal(barrier, inc=1, device_id=(q, lax.rem(p + d, n_snap)), device_id_type=MESH)

    @pl.loop(1, n_space)
    def _(d):
        other = lax.rem(q + d, n_space)
        pl.semaphore_signal(barrier, inc=1, device_id=(other, p), device_id_type=MESH)
        pl.semaphore_signal(barrier, inc=1, device_id=(other, facing * CORES + core), device_id_type=MESH)

    ev_copy = pltpu.make_async_copy(ev_hbm, ev_ref, ev_sem)
    ev_copy.start()
    own = []
    for t in range(2):
        target = lax.rem(row_y + t, 2) * n_far + line
        cols = pl.ds(pl.multiple_of(target * LANES, LANES), LANES)
        own.append(pltpu.make_async_copy(v_hbm.at[:, cols], recv.at[t, line], own_sem.at[t]))
        own[t].start()
    h_copy = pltpu.make_async_copy(h_hbm, h_v, h_sem)
    h_copy.start()

    def s_copy(m):
        rows = pl.ds(m * ROW_TILE, ROW_TILE)
        return pltpu.make_async_copy(s_hbm.at[rows], s_v.at[rows], s_sem.at[m])

    for m in range(tiles_m):
        s_copy(m).start()
    row = lax.broadcasted_iota(jnp.int32, (SUBLANES, LANES), 0)
    ev_copy.wait()
    values = jnp.zeros((SUBLANES, LANES), jnp.float32)
    for r in range(SUBLANES):
        value = ev_ref[((r // COL_BLOCK) * n_space + q) * COL_BLOCK + r % COL_BLOCK]
        values = jnp.where(row == r, value, values)
    scale = lax.rsqrt(values)
    h_copy.wait()
    h_all[far] = h_v[...].astype(jnp.float32)
    for t in range(2):
        own[t].wait()
    pl.semaphore_wait(barrier, n_snap - 1 + 2 * (n_space - 1))

    @pl.loop(1, n_far)
    def _(d):
        other = lax.rem(line + d, n_far)
        for t in range(2):
            target = lax.rem(row_y + t, 2) * n_far + other
            cols = pl.ds(pl.multiple_of(target * LANES, LANES), LANES)
            remote(
                v_hbm.at[:, cols], recv.at[t, line], a_send, a_recv.at[line // groups], q, row_y * n_far + other
            ).start()

    remote(h_all.at[far], h_all.at[far], hy_send, hy_recv, q, facing * CORES + core).start()

    def route_of(o):
        return OWN_ROUTES[o] if o < parts else OVER_ROUTES[o - parts]

    def order_part(i):
        part = part_of(i)
        count = groups - 1 if i == 0 else groups
        drain(recv.at[:, pl.ds(0, count)], a_recv.at[part])
        for t in range(2):
            tiles = swap_lane_groups([recv[t, part * groups + a] for a in range(groups)])
            for k in range(groups):
                cols = slice(k * LANES, (k + 1) * LANES)
                if t == 0:
                    e_all[q, i, :, cols] = tiles[k] * scale
                else:
                    staged[i, :, cols] = tiles[k] * scale

    def send_rows(source, o, sem, space):
        remote(e_all.at[source, o], e_all.at[source, o], g_send, sem, space, p).start()

    def along_x(source, o, sem):
        @pl.loop(1, n_x)
        def _(d):
            send_rows(source, o, sem, 2 * lax.rem(x + d, n_x) + y)

    def send_over(o, sem, space):
        remote(
            staged.at[o - parts], e_all.at[q, o], g_send, sem, space, facing * CORES + core
        ).start()

    def start_chunk(o):
        route = route_of(o)
        if o >= parts:
            if route == "y":
                send_over(o, g_first.at[o], q)
                send_over(o, g_first.at[o], across)
            else:

                @pl.loop(0, n_space)
                def _(d):
                    send_over(o, g_rest.at[o], lax.rem(q + d, n_space))

        elif route == "d":

            @pl.loop(1, n_space)
            def _(d):
                send_rows(q, o, g_rest.at[o], lax.rem(q + d, n_space))

        elif route == "y":
            send_rows(q, o, g_first.at[o], across)
            along_x(q, o, g_rest.at[o])
        else:
            along_x(q, o, g_first.at[o])
            send_rows(q, o, g_rest.at[o], across)

    def relay_chunk(o):
        route = route_of(o)
        if o >= parts and route == "y":
            drain(e_all.at[pl.ds(0, 2), o], g_first.at[o])
            along_x(q, o, g_rest.at[o])
            along_x(across, o, g_rest.at[o])
        elif route == "y":
            drain(e_all.at[0, o], g_first.at[o])
            along_x(across, o, g_rest.at[o])
        elif route == "x" and n_x > 1:
            drain(e_all.at[pl.ds(0, n_x - 1), o], g_first.at[o])

            @pl.loop(1, n_x)
            def _(d):
                send_rows(2 * lax.rem(x + d, n_x) + y, o, g_rest.at[o], across)

    def multiply_chunk(o):
        rest = {"d": n_space - (o < parts), "y": 2 * (n_x - 1), "x": n_x}[route_of(o)]
        if rest:
            drain(e_all.at[pl.ds(0, rest), o], g_rest.at[o])
        weights = mode_rows([e_all[s, o] for s in range(n_space)], n_space // 2).astype(jnp.bfloat16)
        group = group_of(o)

        @pl.loop(0, tiles_m)
        def _(m):
            rows = pl.ds(pl.multiple_of(m * ROW_TILE, ROW_TILE), ROW_TILE)
            parts = []
            for k in range(groups):
                at = pl.multiple_of(k * n_snap * ROW_BLOCK + group * LANES, LANES)
                parts.append(s_v[rows, pl.ds(at, LANES)])
            value = lax.dot_general(
                jnp.concatenate(parts, axis=1), weights, (((1,), (1,)), ((), ())), preferred_element_type=jnp.float32
            )
            if o > 0:
                value = value + acc[rows, :]
            if o < chunks - 1:
                acc[rows, :] = value
            else:
                split = value.reshape(owners, CORES, 2, rows_each // 2, modes)
                mine = pl.ds(m * owners, owners)
                for c in range(CORES):
                    pack[c, mine] = jnp.concatenate([split[:, c, 0], split[:, c, 1]], axis=-1)
                remote(
                    pack.at[1 - core, mine], partner.at[mine], k_send, k_recv.at[m], q, p + 1 - 2 * core
                ).start()

    far_ring = n_z == 8
    reach = (1, 2, n_z - 1, n_z - 2) if far_ring else tuple(range(1, n_z))

    def send_held(kind, source, hop, sem):
        slot = lax.rem(row_y + kind, 2) * n_z + lax.rem(z + source, n_z)
        target = row_y * n_z + lax.rem(z + hop, n_z)
        remote(h_all.at[slot], h_all.at[slot], hz_send, sem, q, target * CORES + core).start()

    def start_held(kind):
        for hop in reach:
            send_held(kind, 0, hop, hz_first.at[kind])

    def relay_held(kind):
        drain(h_all.at[pl.ds(0, len(reach))], hz_first.at[kind])
        if far_ring:
            hops = ((n_z - 2, 1), (2, n_z - 1), (n_z - 2, 2) if kind == 0 else (2, n_z - 2))
            for source, hop in hops:
                send_held(kind, source, hop, hz_rest.at[kind])

    def finish_held():
        if far_ring:
            for kind in range(2):
                drain(h_all.at[pl.ds(0, 3)], hz_rest.at[kind])

    start_held(0)
    for i in range(parts):
        order_part(i)
        start_chunk(i)
        start_chunk(parts + i)
        if i == 0:
            drain(h_all.at[0], hy_recv)
            start_held(1)
    steps = [functools.partial(relay_chunk, o) for i in range(parts) for o in (i, parts + i)]
    steps.insert(HB_OWN if parts > 1 else 0, functools.partial(relay_held, 0))
    steps.insert(HB_FACING if parts > 1 else 1, functools.partial(relay_held, 1))
    for step in steps:
        step()
    for m in range(tiles_m):
        s_copy(m).wait()
    for o in range(chunks):
        multiply_chunk(o)

    @pl.loop(0, tiles_m)
    def _(m):
        mine = pl.ds(m * owners, owners)
        drain(partner.at[mine], k_recv.at[m])
        paired[mine] = pack[core, mine] + partner[mine]

    finish_held()
    partial_value = None
    for s in range(2):
        found = paired[:, :, s * modes : (s + 1) * modes].reshape(n_far * rows_each // 2, modes)
        held = h_all[:, s * rows_each // 2 : (s + 1) * rows_each // 2, :].reshape(n_far * rows_each // 2, h_v.shape[1])
        held = held.astype(jnp.bfloat16)
        upper = found.astype(jnp.bfloat16)
        lower = (found - upper.astype(jnp.float32)).astype(jnp.bfloat16)
        for piece in (upper, lower):
            term = lax.dot_general(piece, held, (((0,), (0,)), ((), ())), preferred_element_type=jnp.float32)
            partial_value = term if partial_value is None else partial_value + term
    wide = h_v.shape[1] // LANES
    for a in range(n_near):
        r, s = a // wide, a % wide
        c_out[a] = partial_value[r * SUBLANES : (r + 1) * SUBLANES, s * LANES : (s + 1) * LANES]

    @pl.loop(1, n_near)
    def _(d):
        other = lax.rem(near + d, n_near)
        remote(c_out.at[other], c_in.at[near], c_send.at[0], c_recv.at[0], *near_id(other)).start()

    @pl.loop(1, n_far)
    def _(d):
        other = lax.rem(far + d, n_far)
        remote(paired.at[other], sums.at[far], r_send, r_recv, q, other * CORES + core).start()

    c_in[near] = c_out[near]
    drain(c_in.at[pl.ds(0, n_near - 1)], c_recv.at[0])
    d_out[...] = jnp.sum(c_in[...], axis=0)

    @pl.loop(1, n_far)
    def _(d):
        other = lax.rem(line + d, n_far)
        remote(d_out, d_in.at[line], c_send.at[1], c_recv.at[1], q, row_y * n_far + other).start()

    d_in[line] = d_out[...]
    sums[far] = paired[far]
    drain(sums.at[pl.ds(0, n_far - 1)], r_recv)
    modes_ref[...] = jnp.sum(sums[...], axis=0)
    drain(d_in.at[pl.ds(0, n_far - 1)], c_recv.at[1])
    f_in[near] = jnp.sum(d_in[...], axis=0) * (1.0 / math.sqrt(total_cells))

    @pl.loop(1, n_near)
    def _(d):
        other = lax.rem(near + d, n_near)
        remote(f_in.at[near], f_in.at[near], c_send.at[2], c_recv.at[2], *near_id(other)).start()

    drain(recv.at[:, pl.ds(0, n_far - 1)], a_send)
    drain(h_all.at[0], hy_send)
    drain(h_all.at[pl.ds(0, 2 * (n_z - 1))], hz_send)
    for o in range(chunks):
        drain(e_all.at[pl.ds(0, n_space - (o < parts)), o], g_send)
    drain(partner, k_send)
    drain(sums.at[pl.ds(0, n_far - 1)], r_send)
    drain(c_out.at[pl.ds(0, n_near - 1)], c_send.at[0])
    drain(d_in.at[pl.ds(0, n_far - 1)], c_send.at[1])
    drain(f_in.at[pl.ds(0, n_near - 1)], c_recv.at[2])
    coef_ref[...] = f_in[...]
    drain(f_in.at[pl.ds(0, n_near - 1)], c_send.at[2])


def place(total_ref, tiles_ref, modes_ref, coef_ref):
    modes = modes_ref.shape[1]
    half = modes_ref.shape[0] // 2
    modes_ref[:half, :] = total_ref[:, :modes].astype(jnp.bfloat16)
    modes_ref[half:, :] = total_ref[:, modes:].astype(jnp.bfloat16)
    wide = coef_ref.shape[1] // LANES
    for a in range(tiles_ref.shape[0]):
        r, s = a // wide, a % wide
        coef_ref[r * SUBLANES : (r + 1) * SUBLANES, s * LANES : (s + 1) * LANES] = tiles_ref[a]


def solution(mesh):
    n_space, n_snap = mesh.shape["space"], mesh.shape["snap"]

    def per_device(snapshots, vectors_cyclic, eigen_values, held_out):
        cells, snaps = snapshots.shape
        modes, held = eigen_values.shape[0], held_out.shape[1]
        rows_each = cells // n_snap
        n_near, n_far = n_space * 2, n_snap // 2
        chunks = n_snap * ROW_BLOCK // LANES
        tile = (SUBLANES, LANES)
        packed = (rows_each // 2, 2 * modes)
        vmem, dma = pltpu.VMEM, pltpu.SemaphoreType.DMA
        f32 = jnp.float32
        total, tiles = pl.pallas_call(
            functools.partial(kernel, n_space, n_snap, cells * n_space),
            out_shape=(vmem(packed, f32), vmem((n_near, *tile), f32)),
            in_specs=[
                pl.BlockSpec(memory_space=pl.ANY),
                pl.BlockSpec(memory_space=pl.ANY),
                pl.BlockSpec(memory_space=pl.ANY),
                pl.BlockSpec(memory_space=pl.ANY),
            ],
            out_specs=[pl.BlockSpec(memory_space=pltpu.VMEM)] * 2,
            scratch_shapes=[
                vmem((cells, snaps), jnp.bfloat16),
                vmem(held_out.shape, jnp.bfloat16),
                pltpu.SMEM((modes,), f32),
                vmem((n_far, *held_out.shape), f32),
                vmem((2, n_far, *tile), f32),
                vmem((chunks // 2, SUBLANES, snaps // chunks), f32),
                vmem((n_space, chunks, SUBLANES, snaps // chunks), f32),
                vmem((cells, modes), f32),
                vmem((CORES, n_far, *packed), f32),
                vmem((n_far, *packed), f32),
                vmem((n_far, *packed), f32),
                vmem((n_far, *packed), f32),
                vmem((n_near, *tile), f32),
                vmem((n_near, *tile), f32),
                vmem(tile, f32),
                vmem((n_far, *tile), f32),
                vmem((n_near, *tile), f32),
                dma((cells // ROW_TILE,)),
                dma,
                dma,
                dma,
                dma((chunks // 2,)),
                dma((2,)),
                dma,
                dma,
                dma,
                dma((2,)),
                dma((2,)),
                dma,
                dma((chunks,)),
                dma((chunks,)),
                dma,
                dma((cells // ROW_TILE,)),
                dma,
                dma,
                dma((3,)),
                dma((3,)),
            ],
            compiler_params=pltpu.CompilerParams(
                collective_id=0, has_side_effects=True, vmem_limit_bytes=VMEM_LIMIT
            ),
        )(snapshots, vectors_cyclic.T, eigen_values, held_out)
        return pl.pallas_call(
            place,
            out_shape=(
                jax.ShapeDtypeStruct((rows_each, modes), jnp.bfloat16),
                jax.ShapeDtypeStruct((modes, held), f32),
            ),
            in_specs=[pl.BlockSpec(memory_space=pltpu.VMEM)] * 2,
            out_specs=[pl.BlockSpec(memory_space=pltpu.VMEM)] * 2,
            compiler_params=pltpu.CompilerParams(vmem_limit_bytes=2 * 1024 * 1024),
        )(total, tiles)

    return jax.shard_map(
        per_device,
        mesh=mesh,
        in_specs=(P("space", "snap"), P("snap", "space"), P(), P(("space", "snap"), None)),
        out_specs=(P(("space", "snap"), None), P()),
        check_vma=False,
    )
```

```python
import functools
import math

import jax
import jax.numpy as jnp
from jax import lax
from jax.experimental import pallas as pl
from jax.experimental.pallas import tpu as pltpu
from jax.sharding import PartitionSpec as P

MESH = pl.DeviceIdType.MESH
ROW_BLOCK = 16
COL_BLOCK = 4
LANES = 128
SUBLANES = 8
CORES = 2
ROW_TILE = 512
VMEM_LIMIT = 57 * 1024 * 1024
OWN_ROUTES = ("x", "x")
OVER_ROUTES = ("y", "y")
STEPS = "r0 r2 h0 h1 r1 r3 m0 m2 m1 m3"
FIRST_STEPS = ""


def swap_lane_groups(tiles):
    count = len(tiles)
    lane = lax.broadcasted_iota(jnp.int32, tiles[0].shape, tiles[0].ndim - 1)
    step = 1
    while step < count:
        low = (lane // (ROW_BLOCK * step)) % 2 == 0
        fresh = list(tiles)
        for a in range(count):
            if a & step:
                continue
            x, y = tiles[a], tiles[a + step]
            fresh[a] = jnp.where(low, x, pltpu.roll(y, ROW_BLOCK * step, y.ndim - 1))
            fresh[a + step] = jnp.where(low, pltpu.roll(x, LANES - ROW_BLOCK * step, x.ndim - 1), y)
        tiles = fresh
        step *= 2
    return tiles


def mode_rows(held_rows, pairs):
    first, second = [], []
    for t in range(pairs):
        even, odd = held_rows[2 * t], held_rows[2 * t + 1]
        upper = lax.broadcasted_iota(jnp.int32, even.shape, 0) < COL_BLOCK
        first.append(jnp.where(upper, even, pltpu.roll(odd, COL_BLOCK, 0)))
        second.append(jnp.where(upper, pltpu.roll(even, COL_BLOCK, 0), odd))
    return jnp.concatenate(first + second, axis=0)


def kernel(
    n_space, n_snap, total_cells,
    s_hbm, v_hbm, ev_hbm, h_hbm,
    modes_ref, coef_ref,
    s_v, h_v, ev_ref, h_all, recv, staged, e_all, acc, pack, partner, paired, sums, c_out, c_in, d_out, d_in, f_in,
    s_sem, h_sem, ev_sem, a_send, a_recv, own_sem, hy_send, hy_recv, hz_send, hz_first, hz_rest, g_send, g_first, g_rest,
    k_send, k_recv, r_send, r_recv, c_send, c_recv,
):
    q, p = lax.axis_index("space"), lax.axis_index("snap")
    core = lax.rem(p, CORES)
    n_near, n_far = n_space * 2, n_snap // 2
    far = p // CORES
    n_x, n_z = n_space // 2, n_far // 2
    x, y = q // 2, lax.rem(q, 2)
    z, row_y = lax.rem(far, n_z), far // n_z
    across = 2 * x + 1 - y
    facing = (1 - row_y) * n_z + z
    near, line = row_y * n_space + q, z * CORES + core
    cells, snaps = s_v.shape
    modes = acc.shape[1]
    groups = LANES // ROW_BLOCK
    chunks = n_snap // groups
    parts = chunks // 2
    rows_each = cells // n_snap
    tiles_m = cells // ROW_TILE
    owners = n_far // tiles_m

    def remote(src, dst, send, arrived, space, snap):
        return pltpu.make_async_remote_copy(
            src_ref=src, dst_ref=dst, send_sem=send, recv_sem=arrived, device_id=(space, snap), device_id_type=MESH
        )

    def drain(view, sem):
        pltpu.make_async_copy(view, view, sem).wait()

    def near_id(a):
        return lax.rem(a, n_space), (a // n_space) * n_far + line

    def part_of(i):
        return lax.rem(line // groups + i, parts)

    def group_of(o):
        t, i = o // parts, o % parts
        return lax.rem(row_y + t, 2) * parts + part_of(i)

    barrier = pltpu.get_barrier_semaphore()

    @pl.loop(1, n_snap)
    def _(d):
        pl.semaphore_signal(barrier, inc=1, device_id=(q, lax.rem(p + d, n_snap)), device_id_type=MESH)

    @pl.loop(1, n_space)
    def _(d):
        other = lax.rem(q + d, n_space)
        pl.semaphore_signal(barrier, inc=1, device_id=(other, p), device_id_type=MESH)
        pl.semaphore_signal(barrier, inc=1, device_id=(other, facing * CORES + core), device_id_type=MESH)

    ev_copy = pltpu.make_async_copy(ev_hbm, ev_ref, ev_sem)
    ev_copy.start()
    own = []
    for t in range(2):
        target = lax.rem(row_y + t, 2) * n_far + line
        cols = pl.ds(pl.multiple_of(target * LANES, LANES), LANES)
        own.append(pltpu.make_async_copy(v_hbm.at[:, cols], recv.at[t, line], own_sem.at[t]))
        own[t].start()
    h_copy = pltpu.make_async_copy(h_hbm, h_v, h_sem)
    h_copy.start()

    def s_copy(m):
        rows = pl.ds(m * ROW_TILE, ROW_TILE)
        return pltpu.make_async_copy(s_hbm.at[rows], s_v.at[rows], s_sem.at[m])

    for m in range(tiles_m):
        s_copy(m).start()
    row = lax.broadcasted_iota(jnp.int32, (SUBLANES, LANES), 0)
    ev_copy.wait()
    values = jnp.zeros((SUBLANES, LANES), jnp.float32)
    for r in range(SUBLANES):
        value = ev_ref[((r // COL_BLOCK) * n_space + q) * COL_BLOCK + r % COL_BLOCK]
        values = jnp.where(row == r, value, values)
    scale = lax.rsqrt(values)
    h_copy.wait()
    h_all[far] = h_v[...].astype(jnp.float32)
    for t in range(2):
        own[t].wait()
    pl.semaphore_wait(barrier, n_snap - 1 + 2 * (n_space - 1))

    @pl.loop(1, n_far)
    def _(d):
        other = lax.rem(line + d, n_far)
        for t in range(2):
            target = lax.rem(row_y + t, 2) * n_far + other
            cols = pl.ds(pl.multiple_of(target * LANES, LANES), LANES)
            remote(
                v_hbm.at[:, cols], recv.at[t, line], a_send, a_recv.at[line // groups], q, row_y * n_far + other
            ).start()

    remote(h_all.at[far], h_all.at[far], hy_send, hy_recv, q, facing * CORES + core).start()

    def route_of(o):
        return OWN_ROUTES[o] if o < parts else OVER_ROUTES[o - parts]

    def order_part(i):
        part = part_of(i)
        count = groups - 1 if i == 0 else groups
        drain(recv.at[:, pl.ds(0, count)], a_recv.at[part])
        for t in range(2):
            tiles = swap_lane_groups([recv[t, part * groups + a] for a in range(groups)])
            for k in range(groups):
                cols = slice(k * LANES, (k + 1) * LANES)
                if t == 0:
                    e_all[q, i, :, cols] = tiles[k] * scale
                else:
                    staged[i, :, cols] = tiles[k] * scale

    def send_rows(source, o, sem, space):
        remote(e_all.at[source, o], e_all.at[source, o], g_send, sem, space, p).start()

    def along_x(source, o, sem):
        @pl.loop(1, n_x)
        def _(d):
            send_rows(source, o, sem, 2 * lax.rem(x + d, n_x) + y)

    def send_over(o, sem, space):
        remote(
            staged.at[o - parts], e_all.at[q, o], g_send, sem, space, facing * CORES + core
        ).start()

    def start_chunk(o):
        route = route_of(o)
        if o >= parts:
            if route == "y":
                send_over(o, g_first.at[o], q)
                send_over(o, g_first.at[o], across)
            else:

                @pl.loop(0, n_space)
                def _(d):
                    send_over(o, g_rest.at[o], lax.rem(q + d, n_space))

        elif route == "d":

            @pl.loop(1, n_space)
            def _(d):
                send_rows(q, o, g_rest.at[o], lax.rem(q + d, n_space))

        elif route == "y":
            send_rows(q, o, g_first.at[o], across)
            along_x(q, o, g_rest.at[o])
        else:
            along_x(q, o, g_first.at[o])
            send_rows(q, o, g_rest.at[o], across)

    def relay_chunk(o):
        route = route_of(o)
        if o >= parts and route == "y":
            drain(e_all.at[pl.ds(0, 2), o], g_first.at[o])
            along_x(q, o, g_rest.at[o])
            along_x(across, o, g_rest.at[o])
        elif route == "y":
            drain(e_all.at[0, o], g_first.at[o])
            along_x(across, o, g_rest.at[o])
        elif route == "x" and n_x > 1:
            drain(e_all.at[pl.ds(0, n_x - 1), o], g_first.at[o])

            @pl.loop(1, n_x)
            def _(d):
                send_rows(2 * lax.rem(x + d, n_x) + y, o, g_rest.at[o], across)

    def multiply_chunk(o, first, last):
        rest = {"d": n_space - (o < parts), "y": 2 * (n_x - 1), "x": n_x}[route_of(o)]
        if rest:
            drain(e_all.at[pl.ds(0, rest), o], g_rest.at[o])
        weights = mode_rows([e_all[s, o] for s in range(n_space)], n_space // 2).astype(jnp.bfloat16)
        group = group_of(o)

        @pl.loop(0, tiles_m)
        def _(m):
            rows = pl.ds(pl.multiple_of(m * ROW_TILE, ROW_TILE), ROW_TILE)
            parts = []
            for k in range(groups):
                at = pl.multiple_of(k * n_snap * ROW_BLOCK + group * LANES, LANES)
                parts.append(s_v[rows, pl.ds(at, LANES)])
            value = lax.dot_general(
                jnp.concatenate(parts, axis=1), weights, (((1,), (1,)), ((), ())), preferred_element_type=jnp.float32
            )
            if not first:
                value = value + acc[rows, :]
            if not last:
                acc[rows, :] = value
            else:
                split = value.reshape(owners, CORES, 2, rows_each // 2, modes)
                mine = pl.ds(m * owners, owners)
                for c in range(CORES):
                    pack[c, mine] = jnp.concatenate([split[:, c, 0], split[:, c, 1]], axis=-1)
                remote(
                    pack.at[1 - core, mine], partner.at[mine], k_send, k_recv.at[m], q, p + 1 - 2 * core
                ).start()

    far_ring = n_z == 8
    reach = (1, 2, n_z - 1, n_z - 2) if far_ring else tuple(range(1, n_z))

    def send_held(kind, source, hop, sem):
        slot = lax.rem(row_y + kind, 2) * n_z + lax.rem(z + source, n_z)
        target = row_y * n_z + lax.rem(z + hop, n_z)
        remote(h_all.at[slot], h_all.at[slot], hz_send, sem, q, target * CORES + core).start()

    def start_held(kind):
        for hop in reach:
            send_held(kind, 0, hop, hz_first.at[kind])

    def relay_held(kind):
        drain(h_all.at[pl.ds(0, len(reach))], hz_first.at[kind])
        if far_ring:
            hops = ((n_z - 2, 1), (2, n_z - 1), (n_z - 2, 2) if kind == 0 else (2, n_z - 2))
            for source, hop in hops:
                send_held(kind, source, hop, hz_rest.at[kind])

    def finish_held():
        if far_ring:
            for kind in range(2):
                drain(h_all.at[pl.ds(0, 3)], hz_rest.at[kind])

    def run(steps):
        for name in steps.split():
            at = int(name[1])
            if name[0] == "h":
                relay_held(at)
            elif at < chunks and name[0] == "r":
                relay_chunk(at)
            elif at < chunks:
                if not done:
                    for m in range(tiles_m):
                        s_copy(m).wait()
                done.append(at)
                multiply_chunk(at, len(done) == 1, len(done) == chunks)

    done = []
    start_held(0)
    for i in range(parts):
        order_part(i)
        start_chunk(i)
        start_chunk(parts + i)
        if i == 0:
            drain(h_all.at[0], hy_recv)
            start_held(1)
            if parts > 1:
                run(FIRST_STEPS)
    run(STEPS)

    @pl.loop(0, tiles_m)
    def _(m):
        mine = pl.ds(m * owners, owners)
        drain(partner.at[mine], k_recv.at[m])
        paired[mine] = pack[core, mine] + partner[mine]

    finish_held()
    partial_value = None
    for s in range(2):
        found = paired[:, :, s * modes : (s + 1) * modes].reshape(n_far * rows_each // 2, modes)
        held = h_all[:, s * rows_each // 2 : (s + 1) * rows_each // 2, :].reshape(n_far * rows_each // 2, h_v.shape[1])
        held = held.astype(jnp.bfloat16)
        upper = found.astype(jnp.bfloat16)
        lower = (found - upper.astype(jnp.float32)).astype(jnp.bfloat16)
        for piece in (upper, lower):
            term = lax.dot_general(piece, held, (((0,), (0,)), ((), ())), preferred_element_type=jnp.float32)
            partial_value = term if partial_value is None else partial_value + term
    wide = h_v.shape[1] // LANES
    for a in range(n_near):
        r, s = a // wide, a % wide
        c_out[a] = partial_value[r * SUBLANES : (r + 1) * SUBLANES, s * LANES : (s + 1) * LANES]

    @pl.loop(1, n_near)
    def _(d):
        other = lax.rem(near + d, n_near)
        remote(c_out.at[other], c_in.at[near], c_send.at[0], c_recv.at[0], *near_id(other)).start()

    @pl.loop(1, n_far)
    def _(d):
        other = lax.rem(far + d, n_far)
        remote(paired.at[other], sums.at[far], r_send, r_recv, q, other * CORES + core).start()

    c_in[near] = c_out[near]
    drain(c_in.at[pl.ds(0, n_near - 1)], c_recv.at[0])
    d_out[...] = jnp.sum(c_in[...], axis=0)

    @pl.loop(1, n_far)
    def _(d):
        other = lax.rem(line + d, n_far)
        remote(d_out, d_in.at[line], c_send.at[1], c_recv.at[1], q, row_y * n_far + other).start()

    d_in[line] = d_out[...]
    sums[far] = paired[far]
    drain(sums.at[pl.ds(0, n_far - 1)], r_recv)
    modes_ref[...] = jnp.sum(sums[...], axis=0)
    drain(d_in.at[pl.ds(0, n_far - 1)], c_recv.at[1])
    f_in[near] = jnp.sum(d_in[...], axis=0) * (1.0 / math.sqrt(total_cells))

    @pl.loop(1, n_near)
    def _(d):
        other = lax.rem(near + d, n_near)
        remote(f_in.at[near], f_in.at[near], c_send.at[2], c_recv.at[2], *near_id(other)).start()

    drain(recv.at[:, pl.ds(0, n_far - 1)], a_send)
    drain(h_all.at[0], hy_send)
    drain(h_all.at[pl.ds(0, 2 * (n_z - 1))], hz_send)
    for o in range(chunks):
        drain(e_all.at[pl.ds(0, n_space - (o < parts)), o], g_send)
    drain(partner, k_send)
    drain(sums.at[pl.ds(0, n_far - 1)], r_send)
    drain(c_out.at[pl.ds(0, n_near - 1)], c_send.at[0])
    drain(d_in.at[pl.ds(0, n_far - 1)], c_send.at[1])
    drain(f_in.at[pl.ds(0, n_near - 1)], c_recv.at[2])
    coef_ref[...] = f_in[...]
    drain(f_in.at[pl.ds(0, n_near - 1)], c_send.at[2])


def place(total_ref, tiles_ref, modes_ref, coef_ref):
    modes = modes_ref.shape[1]
    half = modes_ref.shape[0] // 2
    modes_ref[:half, :] = total_ref[:, :modes].astype(jnp.bfloat16)
    modes_ref[half:, :] = total_ref[:, modes:].astype(jnp.bfloat16)
    wide = coef_ref.shape[1] // LANES
    for a in range(tiles_ref.shape[0]):
        r, s = a // wide, a % wide
        coef_ref[r * SUBLANES : (r + 1) * SUBLANES, s * LANES : (s + 1) * LANES] = tiles_ref[a]


def solution(mesh):
    n_space, n_snap = mesh.shape["space"], mesh.shape["snap"]

    def per_device(snapshots, vectors_cyclic, eigen_values, held_out):
        cells, snaps = snapshots.shape
        modes, held = eigen_values.shape[0], held_out.shape[1]
        rows_each = cells // n_snap
        n_near, n_far = n_space * 2, n_snap // 2
        chunks = n_snap * ROW_BLOCK // LANES
        tile = (SUBLANES, LANES)
        packed = (rows_each // 2, 2 * modes)
        vmem, dma = pltpu.VMEM, pltpu.SemaphoreType.DMA
        f32 = jnp.float32
        total, tiles = pl.pallas_call(
            functools.partial(kernel, n_space, n_snap, cells * n_space),
            out_shape=(vmem(packed, f32), vmem((n_near, *tile), f32)),
            in_specs=[
                pl.BlockSpec(memory_space=pl.ANY),
                pl.BlockSpec(memory_space=pl.ANY),
                pl.BlockSpec(memory_space=pl.ANY),
                pl.BlockSpec(memory_space=pl.ANY),
            ],
            out_specs=[pl.BlockSpec(memory_space=pltpu.VMEM)] * 2,
            scratch_shapes=[
                vmem((cells, snaps), jnp.bfloat16),
                vmem(held_out.shape, jnp.bfloat16),
                pltpu.SMEM((modes,), f32),
                vmem((n_far, *held_out.shape), f32),
                vmem((2, n_far, *tile), f32),
                vmem((chunks // 2, SUBLANES, snaps // chunks), f32),
                vmem((n_space, chunks, SUBLANES, snaps // chunks), f32),
                vmem((cells, modes), f32),
                vmem((CORES, n_far, *packed), f32),
                vmem((n_far, *packed), f32),
                vmem((n_far, *packed), f32),
                vmem((n_far, *packed), f32),
                vmem((n_near, *tile), f32),
                vmem((n_near, *tile), f32),
                vmem(tile, f32),
                vmem((n_far, *tile), f32),
                vmem((n_near, *tile), f32),
                dma((cells // ROW_TILE,)),
                dma,
                dma,
                dma,
                dma((chunks // 2,)),
                dma((2,)),
                dma,
                dma,
                dma,
                dma((2,)),
                dma((2,)),
                dma,
                dma((chunks,)),
                dma((chunks,)),
                dma,
                dma((cells // ROW_TILE,)),
                dma,
                dma,
                dma((3,)),
                dma((3,)),
            ],
            compiler_params=pltpu.CompilerParams(
                collective_id=0, has_side_effects=True, vmem_limit_bytes=VMEM_LIMIT
            ),
        )(snapshots, vectors_cyclic.T, eigen_values, held_out)
        return pl.pallas_call(
            place,
            out_shape=(
                jax.ShapeDtypeStruct((rows_each, modes), jnp.bfloat16),
                jax.ShapeDtypeStruct((modes, held), f32),
            ),
            in_specs=[pl.BlockSpec(memory_space=pltpu.VMEM)] * 2,
            out_specs=[pl.BlockSpec(memory_space=pltpu.VMEM)] * 2,
            compiler_params=pltpu.CompilerParams(vmem_limit_bytes=2 * 1024 * 1024),
        )(total, tiles)

    return jax.shard_map(
        per_device,
        mesh=mesh,
        in_specs=(P("space", "snap"), P("snap", "space"), P(), P(("space", "snap"), None)),
        out_specs=(P(("space", "snap"), None), P()),
        check_vma=False,
    )
```

```python
import functools
import math

import jax
import jax.numpy as jnp
from jax import lax
from jax.experimental import pallas as pl
from jax.experimental.pallas import tpu as pltpu
from jax.sharding import PartitionSpec as P

MESH = pl.DeviceIdType.MESH
ROW_BLOCK = 16
COL_BLOCK = 4
LANES = 128
SUBLANES = 8
CORES = 2
ROW_TILE = 512
VMEM_LIMIT = 57 * 1024 * 1024
OWN_ROUTES = ("x", "x")
OVER_ROUTES = ("y", "y")
STEPS = ("r0", "r2", "h0", "h1", "r1", "r3", "m0", "m2", "m1", "m3")


def swap_lane_groups(tiles):
    count = len(tiles)
    lane = lax.broadcasted_iota(jnp.int32, tiles[0].shape, tiles[0].ndim - 1)
    step = 1
    while step < count:
        low = (lane // (ROW_BLOCK * step)) % 2 == 0
        fresh = list(tiles)
        for a in range(count):
            if a & step:
                continue
            x, y = tiles[a], tiles[a + step]
            fresh[a] = jnp.where(low, x, pltpu.roll(y, ROW_BLOCK * step, y.ndim - 1))
            fresh[a + step] = jnp.where(low, pltpu.roll(x, LANES - ROW_BLOCK * step, x.ndim - 1), y)
        tiles = fresh
        step *= 2
    return tiles


def mode_rows(held_rows, pairs):
    first, second = [], []
    for t in range(pairs):
        even, odd = held_rows[2 * t], held_rows[2 * t + 1]
        upper = lax.broadcasted_iota(jnp.int32, even.shape, 0) < COL_BLOCK
        first.append(jnp.where(upper, even, pltpu.roll(odd, COL_BLOCK, 0)))
        second.append(jnp.where(upper, pltpu.roll(even, COL_BLOCK, 0), odd))
    return jnp.concatenate(first + second, axis=0)


def kernel(
    n_space, n_snap, total_cells,
    s_hbm, v_hbm, ev_hbm, h_hbm,
    modes_ref, coef_ref,
    s_v, h_v, v_v, ev_ref, h_all, recv, staged, e_all, acc, pack, partner, paired, sums, c_out, c_in, d_out, d_in, f_in,
    s_sem, h_sem, v_sem, ev_sem, a_send, a_recv, own_sem, hy_send, hy_recv, hz_send, hz_first, hz_rest, g_send, g_first, g_rest,
    k_send, k_recv, r_send, r_recv, c_send, c_recv,
):
    q, p = lax.axis_index("space"), lax.axis_index("snap")
    core = lax.rem(p, CORES)
    n_near, n_far = n_space * 2, n_snap // 2
    far = p // CORES
    n_x, n_z = n_space // 2, n_far // 2
    x, y = q // 2, lax.rem(q, 2)
    z, row_y = lax.rem(far, n_z), far // n_z
    across = 2 * x + 1 - y
    facing = (1 - row_y) * n_z + z
    near, line = row_y * n_space + q, z * CORES + core
    cells, snaps = s_v.shape
    modes = acc.shape[1]
    groups = LANES // ROW_BLOCK
    chunks = n_snap // groups
    parts = chunks // 2
    rows_each = cells // n_snap
    tiles_m = cells // ROW_TILE
    owners = n_far // tiles_m

    def remote(src, dst, send, arrived, space, snap):
        return pltpu.make_async_remote_copy(
            src_ref=src, dst_ref=dst, send_sem=send, recv_sem=arrived, device_id=(space, snap), device_id_type=MESH
        )

    def drain(view, sem):
        pltpu.make_async_copy(view, view, sem).wait()

    def near_id(a):
        return lax.rem(a, n_space), (a // n_space) * n_far + line

    def part_of(i):
        return lax.rem(line // groups + i, parts)

    def group_of(o):
        t, i = o // parts, o % parts
        return lax.rem(row_y + t, 2) * parts + part_of(i)

    barrier = pltpu.get_barrier_semaphore()

    @pl.loop(1, n_snap)
    def _(d):
        pl.semaphore_signal(barrier, inc=1, device_id=(q, lax.rem(p + d, n_snap)), device_id_type=MESH)

    @pl.loop(1, n_space)
    def _(d):
        other = lax.rem(q + d, n_space)
        pl.semaphore_signal(barrier, inc=1, device_id=(other, p), device_id_type=MESH)
        pl.semaphore_signal(barrier, inc=1, device_id=(other, facing * CORES + core), device_id_type=MESH)

    ev_copy = pltpu.make_async_copy(ev_hbm, ev_ref, ev_sem)
    ev_copy.start()
    v_copy = pltpu.make_async_copy(v_hbm, v_v, v_sem)
    v_copy.start()
    own = []
    for t in range(2):
        target = lax.rem(row_y + t, 2) * n_far + line
        cols = pl.ds(pl.multiple_of(target * LANES, LANES), LANES)
        own.append(pltpu.make_async_copy(v_hbm.at[:, cols], recv.at[t, line], own_sem.at[t]))
        own[t].start()
    h_copy = pltpu.make_async_copy(h_hbm, h_v, h_sem)
    h_copy.start()

    def s_copy(m):
        rows = pl.ds(m * ROW_TILE, ROW_TILE)
        return pltpu.make_async_copy(s_hbm.at[rows], s_v.at[rows], s_sem.at[m])

    row = lax.broadcasted_iota(jnp.int32, (SUBLANES, LANES), 0)
    ev_copy.wait()
    values = jnp.zeros((SUBLANES, LANES), jnp.float32)
    for r in range(SUBLANES):
        value = ev_ref[((r // COL_BLOCK) * n_space + q) * COL_BLOCK + r % COL_BLOCK]
        values = jnp.where(row == r, value, values)
    scale = lax.rsqrt(values)
    h_copy.wait()
    h_all[far] = h_v[...].astype(jnp.float32)
    for t in range(2):
        own[t].wait()
    v_copy.wait()
    pl.semaphore_wait(barrier, n_snap - 1 + 2 * (n_space - 1))

    @pl.loop(1, n_far)
    def _(d):
        other = lax.rem(line + d, n_far)
        for t in range(2):
            target = lax.rem(row_y + t, 2) * n_far + other
            cols = pl.ds(pl.multiple_of(target * LANES, LANES), LANES)
            remote(
                v_v.at[:, cols], recv.at[t, line], a_send, a_recv.at[line // groups], q, row_y * n_far + other
            ).start()

    remote(h_all.at[far], h_all.at[far], hy_send, hy_recv, q, facing * CORES + core).start()

    def route_of(o):
        return OWN_ROUTES[o] if o < parts else OVER_ROUTES[o - parts]

    def order_part(i):
        part = part_of(i)
        count = groups - 1 if i == 0 else groups
        drain(recv.at[:, pl.ds(0, count)], a_recv.at[part])
        for t in range(2):
            tiles = swap_lane_groups([recv[t, part * groups + a] for a in range(groups)])
            for k in range(groups):
                cols = slice(k * LANES, (k + 1) * LANES)
                if t == 0:
                    e_all[q, i, :, cols] = tiles[k] * scale
                else:
                    staged[i, :, cols] = tiles[k] * scale

    def send_rows(source, o, sem, space):
        remote(e_all.at[source, o], e_all.at[source, o], g_send, sem, space, p).start()

    def along_x(source, o, sem):
        @pl.loop(1, n_x)
        def _(d):
            send_rows(source, o, sem, 2 * lax.rem(x + d, n_x) + y)

    def send_over(o, sem, space):
        remote(
            staged.at[o - parts], e_all.at[q, o], g_send, sem, space, facing * CORES + core
        ).start()

    def start_chunk(o):
        route = route_of(o)
        if o >= parts:
            if route == "y":
                send_over(o, g_first.at[o], q)
                send_over(o, g_first.at[o], across)
            else:

                @pl.loop(0, n_space)
                def _(d):
                    send_over(o, g_rest.at[o], lax.rem(q + d, n_space))

        elif route == "d":

            @pl.loop(1, n_space)
            def _(d):
                send_rows(q, o, g_rest.at[o], lax.rem(q + d, n_space))

        elif route == "y":
            send_rows(q, o, g_first.at[o], across)
            along_x(q, o, g_rest.at[o])
        else:
            along_x(q, o, g_first.at[o])
            send_rows(q, o, g_rest.at[o], across)

    def relay_chunk(o):
        route = route_of(o)
        if o >= parts and route == "y":
            drain(e_all.at[pl.ds(0, 2), o], g_first.at[o])
            along_x(q, o, g_rest.at[o])
            along_x(across, o, g_rest.at[o])
        elif route == "y":
            drain(e_all.at[0, o], g_first.at[o])
            along_x(across, o, g_rest.at[o])
        elif route == "x" and n_x > 1:
            drain(e_all.at[pl.ds(0, n_x - 1), o], g_first.at[o])

            @pl.loop(1, n_x)
            def _(d):
                send_rows(2 * lax.rem(x + d, n_x) + y, o, g_rest.at[o], across)

    def multiply_chunk(o, first, last):
        rest = {"d": n_space - (o < parts), "y": 2 * (n_x - 1), "x": n_x}[route_of(o)]
        if rest:
            drain(e_all.at[pl.ds(0, rest), o], g_rest.at[o])
        weights = mode_rows([e_all[s, o] for s in range(n_space)], n_space // 2).astype(jnp.bfloat16)
        group = group_of(o)

        @pl.loop(0, tiles_m)
        def _(m):
            rows = pl.ds(pl.multiple_of(m * ROW_TILE, ROW_TILE), ROW_TILE)
            parts = []
            for k in range(groups):
                at = pl.multiple_of(k * n_snap * ROW_BLOCK + group * LANES, LANES)
                parts.append(s_v[rows, pl.ds(at, LANES)])
            value = lax.dot_general(
                jnp.concatenate(parts, axis=1), weights, (((1,), (1,)), ((), ())), preferred_element_type=jnp.float32
            )
            if not first:
                value = value + acc[rows, :]
            if not last:
                acc[rows, :] = value
            else:
                split = value.reshape(owners, CORES, 2, rows_each // 2, modes)
                mine = pl.ds(m * owners, owners)
                for c in range(CORES):
                    pack[c, mine] = jnp.concatenate([split[:, c, 0], split[:, c, 1]], axis=-1)
                remote(
                    pack.at[1 - core, mine], partner.at[mine], k_send, k_recv.at[m], q, p + 1 - 2 * core
                ).start()

    far_ring = n_z == 8
    reach = (1, 2, n_z - 1, n_z - 2) if far_ring else tuple(range(1, n_z))

    def send_held(kind, source, hop, sem):
        slot = lax.rem(row_y + kind, 2) * n_z + lax.rem(z + source, n_z)
        target = row_y * n_z + lax.rem(z + hop, n_z)
        remote(h_all.at[slot], h_all.at[slot], hz_send, sem, q, target * CORES + core).start()

    def start_held(kind):
        for hop in reach:
            send_held(kind, 0, hop, hz_first.at[kind])

    def relay_held(kind):
        drain(h_all.at[pl.ds(0, len(reach))], hz_first.at[kind])
        if far_ring:
            hops = ((n_z - 2, 1), (2, n_z - 1), (n_z - 2, 2) if kind == 0 else (2, n_z - 2))
            for source, hop in hops:
                send_held(kind, source, hop, hz_rest.at[kind])

    def finish_held():
        if far_ring:
            for kind in range(2):
                drain(h_all.at[pl.ds(0, 3)], hz_rest.at[kind])

    def run(steps):
        for name in steps:
            at = int(name[1])
            if name[0] == "h":
                relay_held(at)
            elif at < chunks and name[0] == "r":
                relay_chunk(at)
            elif at < chunks:
                if not done:
                    for m in range(tiles_m):
                        s_copy(m).wait()
                done.append(at)
                multiply_chunk(at, len(done) == 1, len(done) == chunks)

    done = []
    start_held(0)
    for i in range(parts):
        order_part(i)
        start_chunk(i)
        start_chunk(parts + i)
        if i == 0:
            for m in range(tiles_m):
                s_copy(m).start()
            drain(h_all.at[0], hy_recv)
            start_held(1)
    run(STEPS)

    @pl.loop(0, tiles_m)
    def _(m):
        mine = pl.ds(m * owners, owners)
        drain(partner.at[mine], k_recv.at[m])
        paired[mine] = pack[core, mine] + partner[mine]

    finish_held()
    partial_value = None
    for s in range(2):
        found = paired[:, :, s * modes : (s + 1) * modes].reshape(n_far * rows_each // 2, modes)
        held = h_all[:, s * rows_each // 2 : (s + 1) * rows_each // 2, :].reshape(n_far * rows_each // 2, h_v.shape[1])
        held = held.astype(jnp.bfloat16)
        upper = found.astype(jnp.bfloat16)
        lower = (found - upper.astype(jnp.float32)).astype(jnp.bfloat16)
        for piece in (upper, lower):
            term = lax.dot_general(piece, held, (((0,), (0,)), ((), ())), preferred_element_type=jnp.float32)
            partial_value = term if partial_value is None else partial_value + term
    wide = h_v.shape[1] // LANES
    for a in range(n_near):
        r, s = a // wide, a % wide
        c_out[a] = partial_value[r * SUBLANES : (r + 1) * SUBLANES, s * LANES : (s + 1) * LANES]

    @pl.loop(1, n_near)
    def _(d):
        other = lax.rem(near + d, n_near)
        remote(c_out.at[other], c_in.at[near], c_send.at[0], c_recv.at[0], *near_id(other)).start()

    @pl.loop(1, n_far)
    def _(d):
        other = lax.rem(far + d, n_far)
        remote(paired.at[other], sums.at[far], r_send, r_recv, q, other * CORES + core).start()

    c_in[near] = c_out[near]
    drain(c_in.at[pl.ds(0, n_near - 1)], c_recv.at[0])
    d_out[...] = jnp.sum(c_in[...], axis=0)

    @pl.loop(1, n_far)
    def _(d):
        other = lax.rem(line + d, n_far)
        remote(d_out, d_in.at[line], c_send.at[1], c_recv.at[1], q, row_y * n_far + other).start()

    d_in[line] = d_out[...]
    sums[far] = paired[far]
    drain(sums.at[pl.ds(0, n_far - 1)], r_recv)
    modes_ref[...] = jnp.sum(sums[...], axis=0)
    drain(d_in.at[pl.ds(0, n_far - 1)], c_recv.at[1])
    f_in[near] = jnp.sum(d_in[...], axis=0) * (1.0 / math.sqrt(total_cells))

    @pl.loop(1, n_near)
    def _(d):
        other = lax.rem(near + d, n_near)
        remote(f_in.at[near], f_in.at[near], c_send.at[2], c_recv.at[2], *near_id(other)).start()

    drain(recv.at[:, pl.ds(0, n_far - 1)], a_send)
    drain(h_all.at[0], hy_send)
    drain(h_all.at[pl.ds(0, 2 * (n_z - 1))], hz_send)
    for o in range(chunks):
        drain(e_all.at[pl.ds(0, n_space - (o < parts)), o], g_send)
    drain(partner, k_send)
    drain(sums.at[pl.ds(0, n_far - 1)], r_send)
    drain(c_out.at[pl.ds(0, n_near - 1)], c_send.at[0])
    drain(d_in.at[pl.ds(0, n_far - 1)], c_send.at[1])
    drain(f_in.at[pl.ds(0, n_near - 1)], c_recv.at[2])
    coef_ref[...] = f_in[...]
    drain(f_in.at[pl.ds(0, n_near - 1)], c_send.at[2])


def place(total_ref, tiles_ref, modes_ref, coef_ref):
    modes = modes_ref.shape[1]
    half = modes_ref.shape[0] // 2
    modes_ref[:half, :] = total_ref[:, :modes].astype(jnp.bfloat16)
    modes_ref[half:, :] = total_ref[:, modes:].astype(jnp.bfloat16)
    wide = coef_ref.shape[1] // LANES
    for a in range(tiles_ref.shape[0]):
        r, s = a // wide, a % wide
        coef_ref[r * SUBLANES : (r + 1) * SUBLANES, s * LANES : (s + 1) * LANES] = tiles_ref[a]


def solution(mesh):
    n_space, n_snap = mesh.shape["space"], mesh.shape["snap"]

    def per_device(snapshots, vectors_cyclic, eigen_values, held_out):
        cells, snaps = snapshots.shape
        modes, held = eigen_values.shape[0], held_out.shape[1]
        rows_each = cells // n_snap
        n_near, n_far = n_space * 2, n_snap // 2
        chunks = n_snap * ROW_BLOCK // LANES
        tile = (SUBLANES, LANES)
        packed = (rows_each // 2, 2 * modes)
        vmem, dma = pltpu.VMEM, pltpu.SemaphoreType.DMA
        f32 = jnp.float32
        total, tiles = pl.pallas_call(
            functools.partial(kernel, n_space, n_snap, cells * n_space),
            out_shape=(vmem(packed, f32), vmem((n_near, *tile), f32)),
            in_specs=[
                pl.BlockSpec(memory_space=pl.ANY),
                pl.BlockSpec(memory_space=pl.ANY),
                pl.BlockSpec(memory_space=pl.ANY),
                pl.BlockSpec(memory_space=pl.ANY),
            ],
            out_specs=[pl.BlockSpec(memory_space=pltpu.VMEM)] * 2,
            scratch_shapes=[
                vmem((cells, snaps), jnp.bfloat16),
                vmem(held_out.shape, jnp.bfloat16),
                vmem((SUBLANES, snaps), f32),
                pltpu.SMEM((modes,), f32),
                vmem((n_far, *held_out.shape), f32),
                vmem((2, n_far, *tile), f32),
                vmem((chunks // 2, SUBLANES, snaps // chunks), f32),
                vmem((n_space, chunks, SUBLANES, snaps // chunks), f32),
                vmem((cells, modes), f32),
                vmem((CORES, n_far, *packed), f32),
                vmem((n_far, *packed), f32),
                vmem((n_far, *packed), f32),
                vmem((n_far, *packed), f32),
                vmem((n_near, *tile), f32),
                vmem((n_near, *tile), f32),
                vmem(tile, f32),
                vmem((n_far, *tile), f32),
                vmem((n_near, *tile), f32),
                dma((cells // ROW_TILE,)),
                dma,
                dma,
                dma,
                dma,
                dma((chunks // 2,)),
                dma((2,)),
                dma,
                dma,
                dma,
                dma((2,)),
                dma((2,)),
                dma,
                dma((chunks,)),
                dma((chunks,)),
                dma,
                dma((cells // ROW_TILE,)),
                dma,
                dma,
                dma((3,)),
                dma((3,)),
            ],
            compiler_params=pltpu.CompilerParams(
                collective_id=0, has_side_effects=True, vmem_limit_bytes=VMEM_LIMIT
            ),
        )(snapshots, vectors_cyclic.T, eigen_values, held_out)
        return pl.pallas_call(
            place,
            out_shape=(
                jax.ShapeDtypeStruct((rows_each, modes), jnp.bfloat16),
                jax.ShapeDtypeStruct((modes, held), f32),
            ),
            in_specs=[pl.BlockSpec(memory_space=pltpu.VMEM)] * 2,
            out_specs=[pl.BlockSpec(memory_space=pltpu.VMEM)] * 2,
            compiler_params=pltpu.CompilerParams(vmem_limit_bytes=2 * 1024 * 1024),
        )(total, tiles)

    return jax.shard_map(
        per_device,
        mesh=mesh,
        in_specs=(P("space", "snap"), P("snap", "space"), P(), P(("space", "snap"), None)),
        out_specs=(P(("space", "snap"), None), P()),
        check_vma=False,
    )
```

```python
import functools
import math

import jax
import jax.numpy as jnp
from jax import lax
from jax.experimental import pallas as pl
from jax.experimental.pallas import tpu as pltpu
from jax.sharding import PartitionSpec as P

MESH = pl.DeviceIdType.MESH
ROW_BLOCK = 16
COL_BLOCK = 4
LANES = 128
SUBLANES = 8
CORES = 2
ROW_TILE = 512
VMEM_LIMIT = 57 * 1024 * 1024
OWN_ROUTES = ("x", "x")
OVER_ROUTES = ("y", "y")
STEPS = ("r0", "r2", "h0", "h1", "r1", "r3", "m0", "m2", "m1", "m3")


def swap_lane_groups(tiles):
    count = len(tiles)
    lane = lax.broadcasted_iota(jnp.int32, tiles[0].shape, tiles[0].ndim - 1)
    step = 1
    while step < count:
        low = (lane // (ROW_BLOCK * step)) % 2 == 0
        fresh = list(tiles)
        for a in range(count):
            if a & step:
                continue
            x, y = tiles[a], tiles[a + step]
            fresh[a] = jnp.where(low, x, pltpu.roll(y, ROW_BLOCK * step, y.ndim - 1))
            fresh[a + step] = jnp.where(low, pltpu.roll(x, LANES - ROW_BLOCK * step, x.ndim - 1), y)
        tiles = fresh
        step *= 2
    return tiles


def mode_rows(held_rows, pairs):
    first, second = [], []
    for t in range(pairs):
        even, odd = held_rows[2 * t], held_rows[2 * t + 1]
        upper = lax.broadcasted_iota(jnp.int32, even.shape, 0) < COL_BLOCK
        first.append(jnp.where(upper, even, pltpu.roll(odd, COL_BLOCK, 0)))
        second.append(jnp.where(upper, pltpu.roll(even, COL_BLOCK, 0), odd))
    return jnp.concatenate(first + second, axis=0)


def kernel(
    n_space, n_snap, total_cells,
    s_hbm, v_hbm, ev_hbm, h_hbm,
    modes_ref, coef_ref,
    s_v, h_v, v_v, ev_ref, h_all, recv, staged, e_all, acc, pack, partner, paired, sums, c_out, c_in, d_out, d_in, f_in,
    s_sem, h_sem, v_sem, ev_sem, a_send, a_recv, own_sem, hy_send, hy_recv, hz_send, hz_first, hz_rest, g_send, g_first, g_rest,
    k_send, k_recv, r_send, r_recv, c_send, c_recv,
):
    q, p = lax.axis_index("space"), lax.axis_index("snap")
    core = lax.rem(p, CORES)
    n_near, n_far = n_space * 2, n_snap // 2
    far = p // CORES
    n_x, n_z = n_space // 2, n_far // 2
    x, y = q // 2, lax.rem(q, 2)
    z, row_y = lax.rem(far, n_z), far // n_z
    across = 2 * x + 1 - y
    facing = (1 - row_y) * n_z + z
    near, line = row_y * n_space + q, z * CORES + core
    cells, snaps = s_v.shape
    modes = acc.shape[1]
    groups = LANES // ROW_BLOCK
    chunks = n_snap // groups
    parts = chunks // 2
    rows_each = cells // n_snap
    tiles_m = cells // ROW_TILE
    owners = n_far // tiles_m

    def remote(src, dst, send, arrived, space, snap):
        return pltpu.make_async_remote_copy(
            src_ref=src, dst_ref=dst, send_sem=send, recv_sem=arrived, device_id=(space, snap), device_id_type=MESH
        )

    def drain(view, sem):
        pltpu.make_async_copy(view, view, sem).wait()

    def near_id(a):
        return lax.rem(a, n_space), (a // n_space) * n_far + line

    def part_of(i):
        return lax.rem(line // groups + i, parts)

    def group_of(o):
        t, i = o // parts, o % parts
        return lax.rem(row_y + t, 2) * parts + part_of(i)

    barrier = pltpu.get_barrier_semaphore()

    @pl.loop(1, n_snap)
    def _(d):
        pl.semaphore_signal(barrier, inc=1, device_id=(q, lax.rem(p + d, n_snap)), device_id_type=MESH)

    @pl.loop(1, n_space)
    def _(d):
        other = lax.rem(q + d, n_space)
        pl.semaphore_signal(barrier, inc=1, device_id=(other, p), device_id_type=MESH)
        pl.semaphore_signal(barrier, inc=1, device_id=(other, facing * CORES + core), device_id_type=MESH)

    ev_copy = pltpu.make_async_copy(ev_hbm, ev_ref, ev_sem)
    ev_copy.start()
    v_copy = pltpu.make_async_copy(v_hbm, v_v, v_sem)
    v_copy.start()
    own = []
    for t in range(2):
        target = lax.rem(row_y + t, 2) * n_far + line
        cols = pl.ds(pl.multiple_of(target * LANES, LANES), LANES)
        own.append(pltpu.make_async_copy(v_hbm.at[:, cols], recv.at[t, line], own_sem.at[t]))
        own[t].start()
    h_copy = pltpu.make_async_copy(h_hbm, h_v, h_sem)
    h_copy.start()

    def s_copy(m):
        rows = pl.ds(m * ROW_TILE, ROW_TILE)
        return pltpu.make_async_copy(s_hbm.at[rows], s_v.at[rows], s_sem.at[m])

    v_copy.wait()
    pl.semaphore_wait(barrier, n_snap - 1 + 2 * (n_space - 1))

    @pl.loop(1, n_far)
    def _(d):
        other = lax.rem(line + d, n_far)
        for t in range(2):
            target = lax.rem(row_y + t, 2) * n_far + other
            cols = pl.ds(pl.multiple_of(target * LANES, LANES), LANES)
            remote(
                v_v.at[:, cols], recv.at[t, line], a_send, a_recv.at[line // groups], q, row_y * n_far + other
            ).start()

    row = lax.broadcasted_iota(jnp.int32, (SUBLANES, LANES), 0)
    ev_copy.wait()
    values = jnp.zeros((SUBLANES, LANES), jnp.float32)
    for r in range(SUBLANES):
        value = ev_ref[((r // COL_BLOCK) * n_space + q) * COL_BLOCK + r % COL_BLOCK]
        values = jnp.where(row == r, value, values)
    scale = lax.rsqrt(values)
    h_copy.wait()
    h_all[far] = h_v[...].astype(jnp.float32)
    for t in range(2):
        own[t].wait()

    remote(h_all.at[far], h_all.at[far], hy_send, hy_recv, q, facing * CORES + core).start()

    def route_of(o):
        return OWN_ROUTES[o] if o < parts else OVER_ROUTES[o - parts]

    def order_part(i):
        part = part_of(i)
        count = groups - 1 if i == 0 else groups
        drain(recv.at[:, pl.ds(0, count)], a_recv.at[part])
        for t in range(2):
            tiles = swap_lane_groups([recv[t, part * groups + a] for a in range(groups)])
            for k in range(groups):
                cols = slice(k * LANES, (k + 1) * LANES)
                if t == 0:
                    e_all[q, i, :, cols] = tiles[k] * scale
                else:
                    staged[i, :, cols] = tiles[k] * scale

    def send_rows(source, o, sem, space):
        remote(e_all.at[source, o], e_all.at[source, o], g_send, sem, space, p).start()

    def along_x(source, o, sem):
        @pl.loop(1, n_x)
        def _(d):
            send_rows(source, o, sem, 2 * lax.rem(x + d, n_x) + y)

    def send_over(o, sem, space):
        remote(
            staged.at[o - parts], e_all.at[q, o], g_send, sem, space, facing * CORES + core
        ).start()

    def start_chunk(o):
        route = route_of(o)
        if o >= parts:
            if route == "y":
                send_over(o, g_first.at[o], q)
                send_over(o, g_first.at[o], across)
            else:

                @pl.loop(0, n_space)
                def _(d):
                    send_over(o, g_rest.at[o], lax.rem(q + d, n_space))

        elif route == "d":

            @pl.loop(1, n_space)
            def _(d):
                send_rows(q, o, g_rest.at[o], lax.rem(q + d, n_space))

        elif route == "y":
            send_rows(q, o, g_first.at[o], across)
            along_x(q, o, g_rest.at[o])
        else:
            along_x(q, o, g_first.at[o])
            send_rows(q, o, g_rest.at[o], across)

    def relay_chunk(o):
        route = route_of(o)
        if o >= parts and route == "y":
            drain(e_all.at[pl.ds(0, 2), o], g_first.at[o])
            along_x(q, o, g_rest.at[o])
            along_x(across, o, g_rest.at[o])
        elif route == "y":
            drain(e_all.at[0, o], g_first.at[o])
            along_x(across, o, g_rest.at[o])
        elif route == "x" and n_x > 1:
            drain(e_all.at[pl.ds(0, n_x - 1), o], g_first.at[o])

            @pl.loop(1, n_x)
            def _(d):
                send_rows(2 * lax.rem(x + d, n_x) + y, o, g_rest.at[o], across)

    def multiply_chunk(o, first, last):
        rest = {"d": n_space - (o < parts), "y": 2 * (n_x - 1), "x": n_x}[route_of(o)]
        if rest:
            drain(e_all.at[pl.ds(0, rest), o], g_rest.at[o])
        weights = mode_rows([e_all[s, o] for s in range(n_space)], n_space // 2).astype(jnp.bfloat16)
        group = group_of(o)

        @pl.loop(0, tiles_m)
        def _(m):
            rows = pl.ds(pl.multiple_of(m * ROW_TILE, ROW_TILE), ROW_TILE)
            parts = []
            for k in range(groups):
                at = pl.multiple_of(k * n_snap * ROW_BLOCK + group * LANES, LANES)
                parts.append(s_v[rows, pl.ds(at, LANES)])
            value = lax.dot_general(
                jnp.concatenate(parts, axis=1), weights, (((1,), (1,)), ((), ())), preferred_element_type=jnp.float32
            )
            if not first:
                value = value + acc[rows, :]
            if not last:
                acc[rows, :] = value
            else:
                split = value.reshape(owners, CORES, 2, rows_each // 2, modes)
                mine = pl.ds(m * owners, owners)
                for c in range(CORES):
                    pack[c, mine] = jnp.concatenate([split[:, c, 0], split[:, c, 1]], axis=-1)
                remote(
                    pack.at[1 - core, mine], partner.at[mine], k_send, k_recv.at[m], q, p + 1 - 2 * core
                ).start()

    far_ring = n_z == 8
    reach = (1, 2, n_z - 1, n_z - 2) if far_ring else tuple(range(1, n_z))

    def send_held(kind, source, hop, sem):
        slot = lax.rem(row_y + kind, 2) * n_z + lax.rem(z + source, n_z)
        target = row_y * n_z + lax.rem(z + hop, n_z)
        remote(h_all.at[slot], h_all.at[slot], hz_send, sem, q, target * CORES + core).start()

    def start_held(kind):
        for hop in reach:
            send_held(kind, 0, hop, hz_first.at[kind])

    def relay_held(kind):
        drain(h_all.at[pl.ds(0, len(reach))], hz_first.at[kind])
        if far_ring:
            hops = ((n_z - 2, 1), (2, n_z - 1), (n_z - 2, 2) if kind == 0 else (2, n_z - 2))
            for source, hop in hops:
                send_held(kind, source, hop, hz_rest.at[kind])

    def finish_held():
        if far_ring:
            for kind in range(2):
                drain(h_all.at[pl.ds(0, 3)], hz_rest.at[kind])

    def run(steps):
        for name in steps:
            at = int(name[1])
            if name[0] == "h":
                relay_held(at)
            elif at < chunks and name[0] == "r":
                relay_chunk(at)
            elif at < chunks:
                if not done:
                    for m in range(tiles_m):
                        s_copy(m).wait()
                done.append(at)
                multiply_chunk(at, len(done) == 1, len(done) == chunks)

    done = []
    start_held(0)
    for i in range(parts):
        order_part(i)
        start_chunk(i)
        start_chunk(parts + i)
        if i == 0:
            for m in range(tiles_m):
                s_copy(m).start()
            drain(h_all.at[0], hy_recv)
            start_held(1)
    run(STEPS)

    @pl.loop(0, tiles_m)
    def _(m):
        mine = pl.ds(m * owners, owners)
        drain(partner.at[mine], k_recv.at[m])
        paired[mine] = pack[core, mine] + partner[mine]

    finish_held()
    partial_value = None
    for s in range(2):
        found = paired[:, :, s * modes : (s + 1) * modes].reshape(n_far * rows_each // 2, modes)
        held = h_all[:, s * rows_each // 2 : (s + 1) * rows_each // 2, :].reshape(n_far * rows_each // 2, h_v.shape[1])
        held = held.astype(jnp.bfloat16)
        upper = found.astype(jnp.bfloat16)
        lower = (found - upper.astype(jnp.float32)).astype(jnp.bfloat16)
        for piece in (upper, lower):
            term = lax.dot_general(piece, held, (((0,), (0,)), ((), ())), preferred_element_type=jnp.float32)
            partial_value = term if partial_value is None else partial_value + term
    wide = h_v.shape[1] // LANES
    for a in range(n_near):
        r, s = a // wide, a % wide
        c_out[a] = partial_value[r * SUBLANES : (r + 1) * SUBLANES, s * LANES : (s + 1) * LANES]

    @pl.loop(1, n_near)
    def _(d):
        other = lax.rem(near + d, n_near)
        remote(c_out.at[other], c_in.at[near], c_send.at[0], c_recv.at[0], *near_id(other)).start()

    @pl.loop(1, n_far)
    def _(d):
        other = lax.rem(far + d, n_far)
        remote(paired.at[other], sums.at[far], r_send, r_recv, q, other * CORES + core).start()

    c_in[near] = c_out[near]
    drain(c_in.at[pl.ds(0, n_near - 1)], c_recv.at[0])
    d_out[...] = jnp.sum(c_in[...], axis=0)

    @pl.loop(1, n_far)
    def _(d):
        other = lax.rem(line + d, n_far)
        remote(d_out, d_in.at[line], c_send.at[1], c_recv.at[1], q, row_y * n_far + other).start()

    d_in[line] = d_out[...]
    sums[far] = paired[far]
    drain(sums.at[pl.ds(0, n_far - 1)], r_recv)
    modes_ref[...] = jnp.sum(sums[...], axis=0)
    drain(d_in.at[pl.ds(0, n_far - 1)], c_recv.at[1])
    f_in[near] = jnp.sum(d_in[...], axis=0) * (1.0 / math.sqrt(total_cells))

    @pl.loop(1, n_near)
    def _(d):
        other = lax.rem(near + d, n_near)
        remote(f_in.at[near], f_in.at[near], c_send.at[2], c_recv.at[2], *near_id(other)).start()

    drain(recv.at[:, pl.ds(0, n_far - 1)], a_send)
    drain(h_all.at[0], hy_send)
    drain(h_all.at[pl.ds(0, 2 * (n_z - 1))], hz_send)
    for o in range(chunks):
        drain(e_all.at[pl.ds(0, n_space - (o < parts)), o], g_send)
    drain(partner, k_send)
    drain(sums.at[pl.ds(0, n_far - 1)], r_send)
    drain(c_out.at[pl.ds(0, n_near - 1)], c_send.at[0])
    drain(d_in.at[pl.ds(0, n_far - 1)], c_send.at[1])
    drain(f_in.at[pl.ds(0, n_near - 1)], c_recv.at[2])
    coef_ref[...] = f_in[...]
    drain(f_in.at[pl.ds(0, n_near - 1)], c_send.at[2])


def place(total_ref, tiles_ref, modes_ref, coef_ref):
    modes = modes_ref.shape[1]
    half = modes_ref.shape[0] // 2
    modes_ref[:half, :] = total_ref[:, :modes].astype(jnp.bfloat16)
    modes_ref[half:, :] = total_ref[:, modes:].astype(jnp.bfloat16)
    wide = coef_ref.shape[1] // LANES
    for a in range(tiles_ref.shape[0]):
        r, s = a // wide, a % wide
        coef_ref[r * SUBLANES : (r + 1) * SUBLANES, s * LANES : (s + 1) * LANES] = tiles_ref[a]


def solution(mesh):
    n_space, n_snap = mesh.shape["space"], mesh.shape["snap"]

    def per_device(snapshots, vectors_cyclic, eigen_values, held_out):
        cells, snaps = snapshots.shape
        modes, held = eigen_values.shape[0], held_out.shape[1]
        rows_each = cells // n_snap
        n_near, n_far = n_space * 2, n_snap // 2
        chunks = n_snap * ROW_BLOCK // LANES
        tile = (SUBLANES, LANES)
        packed = (rows_each // 2, 2 * modes)
        vmem, dma = pltpu.VMEM, pltpu.SemaphoreType.DMA
        f32 = jnp.float32
        total, tiles = pl.pallas_call(
            functools.partial(kernel, n_space, n_snap, cells * n_space),
            out_shape=(vmem(packed, f32), vmem((n_near, *tile), f32)),
            in_specs=[
                pl.BlockSpec(memory_space=pl.ANY),
                pl.BlockSpec(memory_space=pl.ANY),
                pl.BlockSpec(memory_space=pl.ANY),
                pl.BlockSpec(memory_space=pl.ANY),
            ],
            out_specs=[pl.BlockSpec(memory_space=pltpu.VMEM)] * 2,
            scratch_shapes=[
                vmem((cells, snaps), jnp.bfloat16),
                vmem(held_out.shape, jnp.bfloat16),
                vmem((SUBLANES, snaps), f32),
                pltpu.SMEM((modes,), f32),
                vmem((n_far, *held_out.shape), f32),
                vmem((2, n_far, *tile), f32),
                vmem((chunks // 2, SUBLANES, snaps // chunks), f32),
                vmem((n_space, chunks, SUBLANES, snaps // chunks), f32),
                vmem((cells, modes), f32),
                vmem((CORES, n_far, *packed), f32),
                vmem((n_far, *packed), f32),
                vmem((n_far, *packed), f32),
                vmem((n_far, *packed), f32),
                vmem((n_near, *tile), f32),
                vmem((n_near, *tile), f32),
                vmem(tile, f32),
                vmem((n_far, *tile), f32),
                vmem((n_near, *tile), f32),
                dma((cells // ROW_TILE,)),
                dma,
                dma,
                dma,
                dma,
                dma((chunks // 2,)),
                dma((2,)),
                dma,
                dma,
                dma,
                dma((2,)),
                dma((2,)),
                dma,
                dma((chunks,)),
                dma((chunks,)),
                dma,
                dma((cells // ROW_TILE,)),
                dma,
                dma,
                dma((3,)),
                dma((3,)),
            ],
            compiler_params=pltpu.CompilerParams(
                collective_id=0, has_side_effects=True, vmem_limit_bytes=VMEM_LIMIT
            ),
        )(snapshots, vectors_cyclic.T, eigen_values, held_out)
        return pl.pallas_call(
            place,
            out_shape=(
                jax.ShapeDtypeStruct((rows_each, modes), jnp.bfloat16),
                jax.ShapeDtypeStruct((modes, held), f32),
            ),
            in_specs=[pl.BlockSpec(memory_space=pltpu.VMEM)] * 2,
            out_specs=[pl.BlockSpec(memory_space=pltpu.VMEM)] * 2,
            compiler_params=pltpu.CompilerParams(vmem_limit_bytes=2 * 1024 * 1024),
        )(total, tiles)

    return jax.shard_map(
        per_device,
        mesh=mesh,
        in_specs=(P("space", "snap"), P("snap", "space"), P(), P(("space", "snap"), None)),
        out_specs=(P(("space", "snap"), None), P()),
        check_vma=False,
    )
```
